512 devices in a mesh: dp: 16 (over z_hi, x, core), seq: 32 (over y, z_lo).
Axes of the slice: x: 4, y: 4, z: 16 (z_hi: 2, z_lo: 8; z = z_hi * 8 + z_lo), core: 2. Of those that a mesh axis runs over, the one named last changes fastest.
Arguments:
- frames: bfloat16 [16, 8192, 1536], P('dp', 'seq'), may hold values from -6 to 6
- lengths: int32 [16], P('dp'), may hold values from 1 to 8192, 38912 in all
- owner_map: int32 [16, 64], P('dp'), may hold values from 0 to 31, as said below
- norm_gain: float32 [1536], replicated, may hold values from 0.5 to 1.5
- norm_bias: float32 [1536], replicated, may hold values from -3 to 3
- proj_weight: bfloat16 [1536, 3072], P('dp'), may hold values from -0.15625 to 0.15625
- dw_kernel: float32 [31, 1536], replicated, may hold values from -1 to 1
- out_grad: bfloat16 [16, 8192, 1536], P('dp', 'seq'), may hold values from -6 to 6
Outputs:
- activations: bfloat16 [16, 8192, 1536], P('dp', 'seq')
- input_grad: bfloat16 [16, 8192, 1536], P('dp', 'seq')
- kernel_grad: float32 [31, 1536], replicated
- gain_grad: float32 [1536], replicated
- bias_grad: float32 [1536], replicated
The draws below stay inside these ranges and needn't reach their ends.
Inputs may be any that keep to these rules, and one draw needn't show every extreme that they name: The longest utterance has exactly 8192 frames; stored rows from lengths[u] on are padding. owner_map[u, g] = (g + owner_map[u, 0]) mod (32): blocks are dealt in turn to the indices of seq from a starting index drawn per utterance, block g in slot g // 32 of its holder.
All inputs are finite; a program needn't handle non-finite values. No bound on the sum of `lengths` on one device may be relied on, other than what follows from the above.
Results may differ from the reference program's by a relative error of at most 0.0064.
Values may be sent and summed in bfloat16 or wider, within the bound.
No kernel may reach another device: no remote copies, remote signals or barrier semaphores. Data moves between devices by JAX's collectives and lax.ppermute only.
A program may use at most 64 MiB of HBM per device.

```python
import math
import jax
import jax.numpy as jnp
import numpy as np
from jax import lax

D = 1536
KER = 31
BLK = 128
BLK_DEV = 2
HALF = 15
NBLK = 64
FRAMES = 8192
UTTS = 16
N_SEQ = 32


def draw_owner_map(key, part):
    key = jax.random.fold_in(key, 7)
    holders = NBLK // BLK_DEV
    starting = jax.random.randint(key, (UTTS,), 0, holders, dtype=jnp.int32)
    block_ids = jnp.arange(NBLK, dtype=jnp.int32)
    return jnp.mod(block_ids[None, :] + starting[:, None], holders).astype(jnp.int32)


def steps_of(stream_key, extent, split, smallest, top_value):
    def one(dim, blocks):
        draws = jax.random.uniform(jax.random.fold_in(jax.random.fold_in(stream_key, 6), dim), (blocks,), jnp.float32, smallest / len(split), top_value / len(split))
        return jnp.repeat(jnp.exp(draws), extent[dim] // blocks).reshape((-1,) + (1,) * (len(extent) - dim - 1))

    factor_of = one(*split[0])
    for cut in split[1:]:
        factor_of = factor_of * one(*cut)
    return factor_of


def profile(amount, total, limit, skew):
    weights = [(1 << 20) // math.isqrt(rank ** skew) + 1 for rank in range(2, amount + 1)]
    spare, holding = total - limit - (amount - 1), [1] * (amount - 1)
    while spare > 0:
        free = [i for i in range(amount - 1) if holding[i] < limit]
        whole, remaining = sum([weights[i] for i in free]), spare
        for i in free:
            addition = min(limit - holding[i], max(1, remaining * weights[i] // whole), spare)
            holding[i] = holding[i] + addition
            spare = spare - addition
    return np.array([limit] + holding)


def ragged_sizes(rng, amount, total, most, skew):
    if amount == 2:
        one = jax.random.randint(rng, (), max(1, total - most), min(most, total - 1) + 1)
        return jnp.stack([one, total - one])
    sizes = jnp.asarray(profile(amount, total, most, skew), jnp.int32)
    twos = (amount - 1) // 2
    donor, taker = sizes[1:1 + 2 * twos:2], sizes[2:2 + 2 * twos:2]
    slack = jnp.minimum(donor - 1, most - taker)
    shifted = jax.random.randint(jax.random.fold_in(rng, 1), (twos,), 0, 1 << 20) % (slack + 1)
    sizes = sizes.at[1:1 + 2 * twos:2].set(donor - shifted).at[2:2 + 2 * twos:2].set(taker + shifted)
    return sizes[jax.random.permutation(jax.random.fold_in(rng, 2), amount)]


def gaussian(stream_key, shape, width, most, pieces=(), held_as=jnp.bfloat16):
    gain = steps_of(stream_key, shape, pieces, -0.22, 0.18) if pieces else 1.0
    values = jax.random.normal(stream_key, shape, jnp.float32) * width * gain
    return jnp.minimum(jnp.maximum(values, -most), most).astype(held_as)


def setup_inputs(seed: int = 0) -> dict:
    streams_of = jax.random.split(jax.random.key(seed), 9)
    frames = gaussian(streams_of[0], (UTTS, FRAMES, D), 1.0, 6.0, ((0, 16), (1, 32)))
    lengths = ragged_sizes(streams_of[1], UTTS, (UTTS + 3) * FRAMES // 4, FRAMES, 2).astype(jnp.int32)
    owner_map = draw_owner_map(jax.random.fold_in(streams_of[8], 71), 0)
    norm_gain = jnp.clip(1.0 + 0.1 * jax.random.normal(streams_of[3], (D,), jnp.float32), 0.5, 1.5)
    norm_bias = gaussian(streams_of[4], (D,), 0.5, 3.0, (), jnp.float32)
    proj_weight = gaussian(streams_of[5], (D, 2 * D), D ** -0.5, 0.15625, ((0, 16),))
    dw_kernel = gaussian(streams_of[6], (KER, D), KER ** -0.5, 1.0, (), jnp.float32)
    out_grad = gaussian(streams_of[7], (UTTS, FRAMES, D), 1.0, 6.0, ((0, 16), (1, 32)))
    return dict(frames=frames, lengths=lengths, owner_map=owner_map, norm_gain=norm_gain, norm_bias=norm_bias, proj_weight=proj_weight, dw_kernel=dw_kernel, out_grad=out_grad)


epsilon = 1e-05

def to_natural(array_row, order_row):
    return array_row.reshape(NBLK, BLK, -1)[order_row].reshape(FRAMES, -1)

def to_stored(array_row, order_row):
    empty = jnp.zeros((NBLK, BLK, array_row.shape[-1]), array_row.dtype)
    return empty.at[order_row].set(array_row.reshape(NBLK, BLK, -1)).reshape(FRAMES, -1)

def reference(frames, lengths, owner_map, norm_gain, norm_bias, proj_weight, dw_kernel, out_grad):
    block_ids = jnp.arange(NBLK, dtype=jnp.int32)
    order = (owner_map * BLK_DEV + block_ids[None, :] // N_SEQ).astype(jnp.int32)
    natural_x = jax.vmap(to_natural)(frames, order)
    natural_dy = jax.vmap(to_natural)(out_grad, order)

    def per_utterance(packed):
        frames_row, grad_row, length_one = packed
        frame_ids = jnp.arange(FRAMES, dtype=jnp.int32)
        live_mask = (frame_ids < length_one)[:, None]
        wide = frames_row.astype(jnp.float32)
        mean_row = lax.optimization_barrier(jnp.mean(wide, axis=1, keepdims=True))
        centered = wide - mean_row
        inv_std = lax.rsqrt(lax.optimization_barrier(jnp.mean(centered * centered, axis=1, keepdims=True)) + epsilon)
        standard = centered * inv_std
        normed = (standard * norm_gain + norm_bias).astype(jnp.bfloat16)
        hidden = jnp.dot(normed, proj_weight, preferred_element_type=jnp.float32)
        gate_half = hidden[:, :D]
        value_half = hidden[:, D:]
        value_sig = jax.nn.sigmoid(value_half)
        gated = jnp.where(live_mask, gate_half * value_sig, 0.0).astype(jnp.bfloat16)
        padded = jnp.pad(gated, ((HALF, HALF), (0, 0)))
        conv_out = jnp.zeros((FRAMES, D), jnp.float32)
        for kernel_tap in range(KER):
            conv_out = conv_out + padded[kernel_tap:kernel_tap + FRAMES] * dw_kernel[kernel_tap]
        conv_sig = jax.nn.sigmoid(conv_out)
        result = jnp.where(live_mask, conv_out * conv_sig, 0.0).astype(jnp.bfloat16)
        slope = jnp.where(live_mask, grad_row.astype(jnp.float32) * (conv_sig + conv_out * conv_sig * (1.0 - conv_sig)), 0.0).astype(jnp.bfloat16)
        slope_wide = slope.astype(jnp.float32)
        padded_slope = jnp.pad(slope, ((HALF, HALF), (0, 0)))
        kernel_terms = []
        back_sum = jnp.zeros((FRAMES, D), jnp.float32)
        for kernel_tap in range(KER):
            kernel_terms.append(lax.optimization_barrier(jnp.sum(slope_wide * padded[kernel_tap:kernel_tap + FRAMES], axis=0)))
            start_row = 2 * HALF - kernel_tap
            back_sum = back_sum + padded_slope[start_row:start_row + FRAMES] * dw_kernel[kernel_tap]
        back_sum = jnp.where(live_mask, back_sum, 0.0)
        grad_hidden = jnp.concatenate([back_sum * value_sig, back_sum * gate_half * value_sig * (1.0 - value_sig)], axis=1).astype(jnp.bfloat16)
        grad_normed = lax.dot_general(grad_hidden, proj_weight, (((1,), (1,)), ((), ())), preferred_element_type=jnp.float32)
        gain_part = lax.optimization_barrier(jnp.sum(grad_normed * standard, axis=0))
        bias_part = lax.optimization_barrier(jnp.sum(grad_normed, axis=0))
        scaled = grad_normed * norm_gain
        grad_x = inv_std * (scaled - lax.optimization_barrier(jnp.mean(scaled, axis=1, keepdims=True)) - standard * lax.optimization_barrier(jnp.mean(scaled * standard, axis=1, keepdims=True)))
        return (result, grad_x.astype(jnp.bfloat16), jnp.stack(kernel_terms), gain_part, bias_part)
    outputs = lax.map(per_utterance, (natural_x, natural_dy, lengths))
    activations = jax.vmap(to_stored)(outputs[0], order)
    input_grad = jax.vmap(to_stored)(outputs[1], order)
    return (activations, input_grad, lax.optimization_barrier(jnp.sum(outputs[2], axis=0)), lax.optimization_barrier(jnp.sum(outputs[3], axis=0)), lax.optimization_barrier(jnp.sum(outputs[4], axis=0)))
```

```python
import jax
import jax.numpy as jnp
from jax import lax
from jax.experimental import pallas as pl
from jax.experimental.pallas import tpu as pltpu
from jax.sharding import Mesh, PartitionSpec as P

D = 1536
TAPS = 31
BLK = 128
HX = 32
EXT = BLK + 2 * HX
HG = 16
EXG = BLK + 2 * HG
SHARD = 96
QUART = 768
LT = D // 128
SLOT = 40
PACK = 512
EPS = 1e-05
F32 = jnp.float32
BF16 = jnp.bfloat16


def sigmoid(v):
    return 0.5 * jnp.tanh(0.5 * v) + 0.5


def shift(count, by):
    return [(i, (i + by) % count) for i in range(count)]


def fused(sc, x_hbm, og_hbm, hp, hn, gain, bias, dw, own0, own1, own2, own3, oc,
          ya0, ya1, ya2, ya3, yb,
          act_ref, ig_ref, red_ref,
          xe, oge, w, nrm, std, inv, gbuf, abuf, sbuf, slp, wb, kacc, gh, gn,
          xsem, wsem):
    pos, length = sc[0], sc[1]
    zh, xi, ci, yi = sc[2], sc[3], sc[4], sc[5]

    xcopies = []

    def go(src, dst, sem, bag):
        c = pltpu.make_async_copy(src, dst, sem)
        c.start()
        bag.append(c)

    for s in range(2):
        before = jnp.maximum(s - jnp.where(pos == 0, 1, 0), 0)
        after = jnp.minimum(s + jnp.where(pos == 31, 1, 0), 1)
        n = 6 * s
        go(x_hbm.at[pl.ds(s * BLK, BLK)], xe.at[pl.ds(s * EXT + HX, BLK)], xsem.at[n], xcopies)
        go(hp.at[pl.ds(pl.multiple_of(before * HX, HX), HX)], xe.at[pl.ds(s * EXT, HX)], xsem.at[n + 1], xcopies)
        go(hn.at[pl.ds(pl.multiple_of(after * HX, HX), HX)], xe.at[pl.ds(s * EXT + HX + BLK, HX)], xsem.at[n + 2], xcopies)
        go(og_hbm.at[pl.ds(s * BLK, BLK)], oge.at[pl.ds(s * EXG + HG, BLK)], xsem.at[n + 3], xcopies)
        go(hp.at[pl.ds(pl.multiple_of(2 * HX + before * HG, HG), HG)], oge.at[pl.ds(s * EXG, HG)], xsem.at[n + 4], xcopies)
        go(hn.at[pl.ds(pl.multiple_of(2 * HX + after * HG, HG), HG)], oge.at[pl.ds(s * EXG + HG + BLK, HG)], xsem.at[n + 5], xcopies)

    wcopies = []

    def row_of(z, x, c):
        return pl.multiple_of((z * 8 + x * 2 + c) * SHARD, SHARD)

    k = 0
    for r, ref in enumerate((own0, own1, own2, own3)):
        xr = lax.rem(xi + 4 - r, 4)
        go(ref, w.at[pl.ds(row_of(zh, xr, ci), SHARD)], wsem.at[k], wcopies)
        go(oc.at[pl.ds(r * SHARD, SHARD)], w.at[pl.ds(row_of(zh, xr, 1 - ci), SHARD)], wsem.at[k + 1], wcopies)
        k += 2
    for dy, ref in enumerate((ya0, ya1, ya2, ya3)):
        col = pl.multiple_of(lax.rem(yi + 4 - dy, 4) * QUART, QUART)
        for r in range(4):
            xr = lax.rem(xi + 4 - r, 4)
            go(ref.at[pl.ds(r * SHARD, SHARD)], w.at[pl.ds(row_of(1 - zh, xr, ci), SHARD), pl.ds(col, QUART)], wsem.at[k], wcopies)
            go(yb.at[pl.ds((dy * 4 + r) * SHARD, SHARD)], w.at[pl.ds(row_of(1 - zh, xr, 1 - ci), SHARD), pl.ds(col, QUART)], wsem.at[k + 1], wcopies)
            k += 2

    red_ref[...] = jnp.zeros((PACK, 128), F32)
    for c in xcopies:
        c.wait()

    gain_row = gain[...]
    bias_row = bias[...]

    def norm_step(i, carry):
        rows = pl.ds(pl.multiple_of(i * 32, 32), 32)
        v = xe[rows, :].astype(F32)
        mean = jnp.sum(v, axis=1, keepdims=True) * (1.0 / D)
        c = v - mean
        var = jnp.sum(c * c, axis=1, keepdims=True) * (1.0 / D)
        iv = lax.rsqrt(var + EPS)
        st = c * iv
        std[rows, :] = st
        inv[rows, :] = jnp.broadcast_to(iv, (32, 128))
        nrm[rows, :] = (st * gain_row + bias_row).astype(BF16)
        return carry

    lax.fori_loop(0, 2 * EXT // 32, norm_step, 0)

    for c in wcopies:
        c.wait()

    row384 = lax.broadcasted_iota(jnp.int32, (2 * EXT, 128), 0)
    second = row384 >= EXT
    t384 = pos * BLK + jnp.where(second, row384 - EXT + 32 * BLK, row384) - HX
    live384 = (t384 >= 0) & (t384 < length)
    iota16 = lax.broadcasted_iota(jnp.int32, (16, 128), 0)

    def chan_step(j, carry):
        col = pl.multiple_of(j * 256, 256)
        normed = nrm[...]
        a = jnp.dot(normed, w[:, pl.ds(col, 256)], preferred_element_type=F32)
        b = jnp.dot(normed, w[:, pl.ds(D + col, 256)], preferred_element_type=F32)
        sg = sigmoid(b)
        for h in range(2):
            ah = a[:, h * 128:(h + 1) * 128]
            sh = sg[:, h * 128:(h + 1) * 128]
            abuf[h] = ah
            sbuf[h] = sh
            gbuf[h] = jnp.where(live384, ah * sh, 0.0).astype(BF16).astype(F32)

        def tile_step(q, carry2):
            h = q // 2
            s = q % 2
            lane = pl.multiple_of((2 * j + h) * 128, 128)
            first = (pos + 32 * s) * BLK
            ext0 = s * EXT

            @pl.when(s == 0)
            def _():
                for k in range(TAPS):
                    wb[k] = jnp.broadcast_to(dw[pl.ds(k, 1), pl.ds(lane, 128)], (8, 128))
                    kacc[k] = jnp.zeros((8, 128), F32)

            taps = [wb[k] for k in range(TAPS)]
            acc = {}
            done = {}
            for o in range(1, 8 * 19 + 32):
                v = gbuf[h, pl.ds(ext0 + o, 8), :]
                for i in range(20):
                    k = o - 1 - 8 * i
                    if 0 <= k < TAPS:
                        p = v * taps[k]
                        acc[i] = p if k == 0 else acc[i] + p
                        if k == TAPS - 1:
                            done[i] = acc.pop(i)
                            if i % 2 == 1:
                                m = i // 2
                                conv = jnp.concatenate([done.pop(i - 1), done.pop(i)], axis=0)
                                cs = sigmoid(conv)
                                t = iota16 + (first + 16 * m - HG)
                                live = (t >= 0) & (t < length)
                                og = oge[pl.ds(pl.multiple_of(s * EXG + 16 * m, 16), 16), pl.ds(lane, 128)].astype(F32)
                                av = conv * cs
                                sl = jnp.where(live, og * (cs + av * (1.0 - cs)), 0.0).astype(BF16).astype(F32)
                                slp[pl.ds(16 * m, 16), :] = sl
                                if 1 <= m <= 8:
                                    act_ref[pl.ds(pl.multiple_of(s * BLK + 16 * (m - 1), 16), 16), pl.ds(lane, 128)] = (
                                        jnp.where(live, av, 0.0).astype(BF16))

            ks = [kacc[k] for k in range(TAPS)]
            sv = {}
            for o in range(17, 17 + 8 * 15 + TAPS):
                v = gbuf[h, pl.ds(ext0 + o, 8), :]
                for i in range(16):
                    k = o - 17 - 8 * i
                    if 0 <= k < TAPS:
                        if k == 0:
                            sv[i] = slp[pl.ds(16 + 8 * i, 8), :]
                        ks[k] = ks[k] + v * sv[i]
            for k in range(TAPS):
                kacc[k] = ks[k]

            @pl.when(s == 1)
            def _():
                for k in range(TAPS):
                    red_ref[pl.ds((2 * j + h) * SLOT + k, 1), :] = jnp.sum(ks[k], axis=0, keepdims=True)

            acc = {}
            done = {}
            for o in range(1, 8 * 15 + 32):
                v = slp[pl.ds(o, 8), :]
                for i in range(16):
                    k = 31 + 8 * i - o
                    if 0 <= k < TAPS:
                        p = v * taps[k]
                        acc[i] = p if k == TAPS - 1 else acc[i] + p
                        if k == 0:
                            done[i] = acc.pop(i)
                            if i % 2 == 1:
                                m = i // 2
                                back = jnp.concatenate([done.pop(i - 1), done.pop(i)], axis=0)
                                t = iota16 + (first + 16 * m)
                                back = jnp.where(t < length, back, 0.0)
                                rows = pl.ds(pl.multiple_of(ext0 + HX + 16 * m, 16), 16)
                                av = abuf[h, rows, :]
                                sgv = sbuf[h, rows, :]
                                ga = back * sgv
                                out = pl.ds(pl.multiple_of(s * BLK + 16 * m, 16), 16)
                                gh[out, pl.ds(lane, 128)] = ga.astype(BF16)
                                gh[out, pl.ds(D + lane, 128)] = (ga * av * (1.0 - sgv)).astype(BF16)
            return carry2

        lax.fori_loop(0, 4, tile_step, 0)
        return carry

    lax.fori_loop(0, D // 256, chan_step, 0)

    def back_step(n, carry):
        rows = pl.ds(pl.multiple_of(n * 256, 256), 256)
        gn[:, rows] = lax.dot_general(gh[...], w[rows, :], (((1,), (1,)), ((), ())), preferred_element_type=F32)
        return carry

    lax.fori_loop(0, D // 256, back_step, 0)

    def grad_step(i, carry):
        gsum, bsum = carry
        src = pl.ds(pl.multiple_of(jnp.where(i >= 4, EXT - BLK, 0) + HX + i * 32, 32), 32)
        dst = pl.ds(pl.multiple_of(i * 32, 32), 32)
        g = gn[dst, :]
        st = std[src, :]
        gs = g * st
        for q in range(4):
            gsum = gsum + gs[q * 8:(q + 1) * 8]
            bsum = bsum + g[q * 8:(q + 1) * 8]
        sc_ = g * gain_row
        m1 = jnp.sum(sc_, axis=1, keepdims=True) * (1.0 / D)
        m2 = jnp.sum(sc_ * st, axis=1, keepdims=True) * (1.0 / D)
        iv = inv[src, 0:1]
        ig_ref[dst, :] = (iv * (sc_ - m1 - st * m2)).astype(BF16)
        return gsum, bsum

    zero = jnp.zeros((8, D), F32)
    gsum, bsum = lax.fori_loop(0, 8, grad_step, (zero, zero))
    grow = jnp.sum(gsum, axis=0, keepdims=True)
    brow = jnp.sum(bsum, axis=0, keepdims=True)
    for l in range(LT):
        red_ref[l * SLOT + TAPS:l * SLOT + TAPS + 1, :] = grow[:, l * 128:(l + 1) * 128]
        red_ref[l * SLOT + TAPS + 1:l * SLOT + TAPS + 2, :] = brow[:, l * 128:(l + 1) * 128]


def run_fused(scalars, frames, out_grad, hp, hn, gain, bias, dw, pieces):
    any_spec = pl.BlockSpec(memory_space=pl.ANY)
    vm = pl.BlockSpec(memory_space=pltpu.VMEM)
    return pl.pallas_call(
        fused,
        out_shape=(
            jax.ShapeDtypeStruct((2 * BLK, D), BF16),
            jax.ShapeDtypeStruct((2 * BLK, D), BF16),
            jax.ShapeDtypeStruct((PACK, 128), F32),
        ),
        in_specs=[pl.BlockSpec(memory_space=pltpu.SMEM)] + [any_spec] * 4 + [vm] * 3 + [any_spec] * len(pieces),
        out_specs=(vm, vm, vm),
        scratch_shapes=[
            pltpu.VMEM((2 * EXT, D), BF16),
            pltpu.VMEM((2 * EXG, D), BF16),
            pltpu.VMEM((D, 2 * D), BF16),
            pltpu.VMEM((2 * EXT, D), BF16),
            pltpu.VMEM((2 * EXT, D), F32),
            pltpu.VMEM((2 * EXT, 128), F32),
            pltpu.VMEM((2, 2 * EXT, 128), F32),
            pltpu.VMEM((2, 2 * EXT, 128), F32),
            pltpu.VMEM((2, 2 * EXT, 128), F32),
            pltpu.VMEM((EXG, 128), F32),
            pltpu.VMEM((TAPS, 8, 128), F32),
            pltpu.VMEM((TAPS, 8, 128), F32),
            pltpu.VMEM((2 * BLK, 2 * D), BF16),
            pltpu.VMEM((2 * BLK, D), F32),
            pltpu.SemaphoreType.DMA((12,)),
            pltpu.SemaphoreType.DMA((40,)),
        ],
        compiler_params=pltpu.CompilerParams(vmem_limit_bytes=48 * 1024 * 1024),
        cost_estimate=pl.CostEstimate(flops=9_000_000_000, bytes_accessed=14_000_000, transcendentals=2_000_000),
    )(scalars, frames, out_grad, hp, hn, gain, bias, dw, *pieces)


def gather_weight(own):
    yi = lax.axis_index("y")
    quarter = lax.dynamic_slice_in_dim(own, yi * QUART, QUART, axis=1)
    far = lax.ppermute(quarter, "zh", shift(2, 1))
    far = [far] + [lax.ppermute(far, "x", shift(4, d)) for d in (1, 2, 3)]
    far = jnp.concatenate(far, axis=0)
    ya = [far] + [lax.ppermute(far, "y", shift(4, d)) for d in (1, 2, 3)]
    mine = [own] + [lax.ppermute(own, "x", shift(4, d)) for d in (1, 2, 3)]
    oc = lax.ppermute(jnp.concatenate(mine, axis=0), "core", shift(2, 1))
    yb = lax.ppermute(jnp.concatenate(ya, axis=0), "core", shift(2, 1))
    return mine + [oc] + ya + [yb]


def reduce_all(packed):
    plane = ("x", "core", "y")
    parts = lax.all_to_all(packed.reshape(32, PACK // 32, 128), plane, 0, 0)
    mine = jnp.sum(parts, axis=0)
    line = lax.all_to_all(jnp.broadcast_to(mine[None], (16,) + mine.shape), ("zh", "zl"), 0, 0)
    mine = jnp.sum(line, axis=0)
    whole = lax.all_to_all(jnp.broadcast_to(mine[None], (32,) + mine.shape), plane, 0, 0)
    whole = whole.reshape(PACK, 128)[: LT * SLOT].reshape(LT, SLOT, 128)
    whole = jnp.swapaxes(whole, 0, 1).reshape(SLOT, D)
    return whole[:TAPS], whole[TAPS], whole[TAPS + 1]


def on_device(frames, lengths, owner_map, norm_gain, norm_bias, proj_weight, dw_kernel, out_grad):
    idx = lax.axis_index
    x = frames.reshape(2 * BLK, D)
    dy = out_grad.reshape(2 * BLK, D)
    seq = idx("y") * 8 + idx("zl")
    position = jnp.mod(seq - owner_map[0, 0], 32)
    scalars = jnp.stack([position, lengths[0], idx("zh"), idx("x"), idx("core"), idx("y"), position, position]).astype(jnp.int32)

    tails = jnp.concatenate([x[BLK - HX:BLK], x[2 * BLK - HX:], dy[BLK - HG:BLK], dy[2 * BLK - HG:]], axis=0)
    heads = jnp.concatenate([x[:HX], x[BLK:BLK + HX], dy[:HG], dy[BLK:BLK + HG]], axis=0)
    pieces = gather_weight(proj_weight)
    hp = lax.ppermute(tails, ("y", "zl"), shift(32, 1))
    hn = lax.ppermute(heads, ("y", "zl"), shift(32, -1))
    act, ig, packed = run_fused(
        scalars, x, dy, hp, hn, norm_gain.reshape(1, D), norm_bias.reshape(1, D), dw_kernel, pieces)
    kernel_grad, gain_grad, bias_grad = reduce_all(packed)
    return act.reshape(1, 2 * BLK, D), ig.reshape(1, 2 * BLK, D), kernel_grad, gain_grad, bias_grad


def solution(mesh):
    fine = Mesh(mesh.devices.reshape(2, 4, 2, 4, 8), ("zh", "x", "core", "y", "zl"))
    dp, seq = ("zh", "x", "core"), ("y", "zl")
    return jax.shard_map(
        on_device,
        mesh=fine,
        in_specs=(P(dp, seq, None), P(dp), P(dp, None), P(), P(), P(dp, None), P(), P(dp, seq, None)),
        out_specs=(P(dp, seq, None), P(dp, seq, None), P(), P(), P()),
        check_vma=False,
    )
```

```python
import jax
import jax.numpy as jnp
from jax import lax
from jax.experimental import pallas as pl
from jax.experimental.pallas import tpu as pltpu
from jax.sharding import Mesh, PartitionSpec as P

D = 1536
TAPS = 31
BLK = 128
HX = 32
EXT = BLK + 2 * HX
HG = 16
EXG = BLK + 2 * HG
SHARD = 96
HALF = 768
QUART = 768
LT = D // 128
SLOT = 40
PACK = 512
EPS = 1e-05
F32 = jnp.float32
BF16 = jnp.bfloat16


def sigmoid(v):
    return 0.5 * jnp.tanh(0.5 * v) + 0.5


def shift(count, by):
    return [(i, (i + by) % count) for i in range(count)]


def fused(sc, x_hbm, og_hbm, hp, hn, dw, near, ya0, ya1, ya2, ya3, yb0, yb1, yb2, yb3,
          act_ref, ig_ref, red_ref,
          xe, oge, w, nrm, std, inv, gbuf, abuf, sbuf, slp, wb, kacc, gh, gn,
          xsem, wsem):
    pos, length = sc[0], sc[1]
    zh, ci, turn = sc[2], sc[3], sc[4]

    xcopies = []

    def go(src, dst, sem, bag):
        c = pltpu.make_async_copy(src, dst, sem)
        c.start()
        bag.append(c)

    for s in range(2):
        before = jnp.maximum(s - jnp.where(pos == 0, 1, 0), 0)
        after = jnp.minimum(s + jnp.where(pos == 31, 1, 0), 1)
        n = 6 * s
        go(x_hbm.at[pl.ds(s * BLK, BLK)], xe.at[pl.ds(s * EXT + HX, BLK)], xsem.at[n], xcopies)
        go(hp.at[pl.ds(pl.multiple_of(before * HX, HX), HX)], xe.at[pl.ds(s * EXT, HX)], xsem.at[n + 1], xcopies)
        go(hn.at[pl.ds(pl.multiple_of(after * HX, HX), HX)], xe.at[pl.ds(s * EXT + HX + BLK, HX)], xsem.at[n + 2], xcopies)
        go(og_hbm.at[pl.ds(s * BLK, BLK)], oge.at[pl.ds(s * EXG + HG, BLK)], xsem.at[n + 3], xcopies)
        go(hp.at[pl.ds(pl.multiple_of(2 * HX + before * HG, HG), HG)], oge.at[pl.ds(s * EXG, HG)], xsem.at[n + 4], xcopies)
        go(hn.at[pl.ds(pl.multiple_of(2 * HX + after * HG, HG), HG)], oge.at[pl.ds(s * EXG + HG + BLK, HG)], xsem.at[n + 5], xcopies)

    wcopies = []

    def row_of(z, x, c):
        return pl.multiple_of((z * 8 + x * 2 + c) * SHARD, SHARD)

    go(near, w.at[pl.ds(pl.multiple_of(zh * HALF, HALF), HALF)], wsem.at[32], wcopies)
    k = 0
    for d, (ra, rb) in enumerate(((ya0, yb0), (ya1, yb1), (ya2, yb2), (ya3, yb3))):
        col = pl.multiple_of(lax.rem(turn + 4 - d, 4) * QUART, QUART)
        for r in range(4):
            go(ra.at[pl.ds(r * SHARD, SHARD)], w.at[pl.ds(row_of(1 - zh, r, ci), SHARD), pl.ds(col, QUART)], wsem.at[k], wcopies)
            go(rb.at[pl.ds(r * SHARD, SHARD)], w.at[pl.ds(row_of(1 - zh, r, 1 - ci), SHARD), pl.ds(col, QUART)], wsem.at[k + 1], wcopies)
            k += 2

    red_ref[...] = jnp.zeros((PACK, 128), F32)
    for c in xcopies:
        c.wait()

    gain_row = dw[TAPS:TAPS + 1, :]
    bias_row = dw[TAPS + 1:TAPS + 2, :]

    def norm_step(i, carry):
        rows = pl.ds(pl.multiple_of(i * 32, 32), 32)
        v = xe[rows, :].astype(F32)
        mean = jnp.sum(v, axis=1, keepdims=True) * (1.0 / D)
        c = v - mean
        var = jnp.sum(c * c, axis=1, keepdims=True) * (1.0 / D)
        iv = lax.rsqrt(var + EPS)
        st = c * iv
        std[rows, :] = st
        inv[rows, :] = jnp.broadcast_to(iv, (32, 128))
        nrm[rows, :] = (st * gain_row + bias_row).astype(BF16)
        return carry

    lax.fori_loop(0, 2 * EXT // 32, norm_step, 0)

    for c in wcopies:
        c.wait()

    row384 = lax.broadcasted_iota(jnp.int32, (2 * EXT, 128), 0)
    second = row384 >= EXT
    t384 = pos * BLK + jnp.where(second, row384 - EXT + 32 * BLK, row384) - HX
    live384 = (t384 >= 0) & (t384 < length)
    iota16 = lax.broadcasted_iota(jnp.int32, (16, 128), 0)

    def chan_step(j, carry):
        col = pl.multiple_of(j * 256, 256)
        normed = nrm[...]
        a = jnp.dot(normed, w[:, pl.ds(col, 256)], preferred_element_type=F32)
        b = jnp.dot(normed, w[:, pl.ds(D + col, 256)], preferred_element_type=F32)
        sg = sigmoid(b)
        for h in range(2):
            ah = a[:, h * 128:(h + 1) * 128]
            sh = sg[:, h * 128:(h + 1) * 128]
            abuf[h] = ah
            sbuf[h] = sh
            gbuf[h] = jnp.where(live384, ah * sh, 0.0).astype(BF16).astype(F32)

        def tile_step(q, carry2):
            h = q // 2
            s = q % 2
            lane = pl.multiple_of((2 * j + h) * 128, 128)
            first = (pos + 32 * s) * BLK
            ext0 = s * EXT

            @pl.when(s == 0)
            def _():
                for k in range(TAPS):
                    wb[k] = jnp.broadcast_to(dw[pl.ds(k, 1), pl.ds(lane, 128)], (8, 128))
                    kacc[k] = jnp.zeros((8, 128), F32)

            taps = [wb[k] for k in range(TAPS)]
            acc = {}
            done = {}
            for o in range(1, 8 * 19 + 32):
                v = gbuf[h, pl.ds(ext0 + o, 8), :]
                for i in range(20):
                    k = o - 1 - 8 * i
                    if 0 <= k < TAPS:
                        p = v * taps[k]
                        acc[i] = p if k == 0 else acc[i] + p
                        if k == TAPS - 1:
                            done[i] = acc.pop(i)
                            if i % 2 == 1:
                                m = i // 2
                                conv = jnp.concatenate([done.pop(i - 1), done.pop(i)], axis=0)
                                cs = sigmoid(conv)
                                t = iota16 + (first + 16 * m - HG)
                                live = (t >= 0) & (t < length)
                                og = oge[pl.ds(pl.multiple_of(s * EXG + 16 * m, 16), 16), pl.ds(lane, 128)].astype(F32)
                                av = conv * cs
                                sl = jnp.where(live, og * (cs + av * (1.0 - cs)), 0.0).astype(BF16).astype(F32)
                                slp[pl.ds(16 * m, 16), :] = sl
                                if 1 <= m <= 8:
                                    act_ref[pl.ds(pl.multiple_of(s * BLK + 16 * (m - 1), 16), 16), pl.ds(lane, 128)] = (
                                        jnp.where(live, av, 0.0).astype(BF16))

            ks = [kacc[k] for k in range(TAPS)]
            sv = {}
            for o in range(17, 17 + 8 * 15 + TAPS):
                v = gbuf[h, pl.ds(ext0 + o, 8), :]
                for i in range(16):
                    k = o - 17 - 8 * i
                    if 0 <= k < TAPS:
                        if k == 0:
                            sv[i] = slp[pl.ds(16 + 8 * i, 8), :]
                        ks[k] = ks[k] + v * sv[i]
            for k in range(TAPS):
                kacc[k] = ks[k]

            @pl.when(s == 1)
            def _():
                for k in range(TAPS):
                    red_ref[pl.ds((2 * j + h) * SLOT + k, 1), :] = jnp.sum(ks[k], axis=0, keepdims=True)

            acc = {}
            done = {}
            for o in range(1, 8 * 15 + 32):
                v = slp[pl.ds(o, 8), :]
                for i in range(16):
                    k = 31 + 8 * i - o
                    if 0 <= k < TAPS:
                        p = v * taps[k]
                        acc[i] = p if k == TAPS - 1 else acc[i] + p
                        if k == 0:
                            done[i] = acc.pop(i)
                            if i % 2 == 1:
                                m = i // 2
                                back = jnp.concatenate([done.pop(i - 1), done.pop(i)], axis=0)
                                t = iota16 + (first + 16 * m)
                                back = jnp.where(t < length, back, 0.0)
                                rows = pl.ds(pl.multiple_of(ext0 + HX + 16 * m, 16), 16)
                                av = abuf[h, rows, :]
                                sgv = sbuf[h, rows, :]
                                ga = back * sgv
                                out = pl.ds(pl.multiple_of(s * BLK + 16 * m, 16), 16)
                                gh[out, pl.ds(lane, 128)] = ga.astype(BF16)
                                gh[out, pl.ds(D + lane, 128)] = (ga * av * (1.0 - sgv)).astype(BF16)
            return carry2

        lax.fori_loop(0, 4, tile_step, 0)
        return carry

    lax.fori_loop(0, D // 256, chan_step, 0)

    def back_step(n, carry):
        rows = pl.ds(pl.multiple_of(n * 256, 256), 256)
        gn[:, rows] = lax.dot_general(gh[...], w[rows, :], (((1,), (1,)), ((), ())), preferred_element_type=F32)
        return carry

    lax.fori_loop(0, D // 256, back_step, 0)

    def grad_step(i, carry):
        gsum, bsum = carry
        src = pl.ds(pl.multiple_of(jnp.where(i >= 4, EXT - BLK, 0) + HX + i * 32, 32), 32)
        dst = pl.ds(pl.multiple_of(i * 32, 32), 32)
        g = gn[dst, :]
        st = std[src, :]
        gs = g * st
        for q in range(4):
            gsum = gsum + gs[q * 8:(q + 1) * 8]
            bsum = bsum + g[q * 8:(q + 1) * 8]
        sc_ = g * gain_row
        m1 = jnp.sum(sc_, axis=1, keepdims=True) * (1.0 / D)
        m2 = jnp.sum(sc_ * st, axis=1, keepdims=True) * (1.0 / D)
        iv = inv[src, 0:1]
        ig_ref[dst, :] = (iv * (sc_ - m1 - st * m2)).astype(BF16)
        return gsum, bsum

    zero = jnp.zeros((8, D), F32)
    gsum, bsum = lax.fori_loop(0, 8, grad_step, (zero, zero))
    grow = jnp.sum(gsum, axis=0, keepdims=True)
    brow = jnp.sum(bsum, axis=0, keepdims=True)
    for l in range(LT):
        red_ref[l * SLOT + TAPS:l * SLOT + TAPS + 1, :] = grow[:, l * 128:(l + 1) * 128]
        red_ref[l * SLOT + TAPS + 1:l * SLOT + TAPS + 2, :] = brow[:, l * 128:(l + 1) * 128]


def run_fused(scalars, frames, out_grad, hp, hn, params, pieces):
    any_spec = pl.BlockSpec(memory_space=pltpu.HBM)
    vm = pl.BlockSpec(memory_space=pltpu.VMEM)
    return pl.pallas_call(
        fused,
        out_shape=(
            jax.ShapeDtypeStruct((2 * BLK, D), BF16),
            jax.ShapeDtypeStruct((2 * BLK, D), BF16),
            jax.ShapeDtypeStruct((PACK, 128), F32),
        ),
        in_specs=[pl.BlockSpec(memory_space=pltpu.SMEM)] + [any_spec] * 4 + [vm] + [any_spec] * len(pieces),
        out_specs=(vm, vm, vm),
        scratch_shapes=[
            pltpu.VMEM((2 * EXT, D), BF16),
            pltpu.VMEM((2 * EXG, D), BF16),
            pltpu.VMEM((D, 2 * D), BF16),
            pltpu.VMEM((2 * EXT, D), BF16),
            pltpu.VMEM((2 * EXT, D), F32),
            pltpu.VMEM((2 * EXT, 128), F32),
            pltpu.VMEM((2, 2 * EXT, 128), F32),
            pltpu.VMEM((2, 2 * EXT, 128), F32),
            pltpu.VMEM((2, 2 * EXT, 128), F32),
            pltpu.VMEM((EXG, 128), F32),
            pltpu.VMEM((TAPS, 8, 128), F32),
            pltpu.VMEM((TAPS, 8, 128), F32),
            pltpu.VMEM((2 * BLK, 2 * D), BF16),
            pltpu.VMEM((2 * BLK, D), F32),
            pltpu.SemaphoreType.DMA((12,)),
            pltpu.SemaphoreType.DMA((40,)),
        ],
        compiler_params=pltpu.CompilerParams(vmem_limit_bytes=48 * 1024 * 1024),
        cost_estimate=pl.CostEstimate(flops=9_000_000_000, bytes_accessed=14_000_000, transcendentals=2_000_000),
    )(scalars, frames, out_grad, hp, hn, params, *pieces)


def take_rims(x, g, tails, heads, sem):
    copies = []
    for dst, fx, fg in ((tails, BLK - HX, BLK - HG), (heads, 0, 0)):
        for s in range(2):
            copies.append(pltpu.make_async_copy(x.at[pl.ds(s * BLK + fx, HX)], dst.at[pl.ds(s * HX, HX)], sem.at[len(copies)]))
            copies.append(pltpu.make_async_copy(g.at[pl.ds(s * BLK + fg, HG)], dst.at[pl.ds(2 * HX + s * HG, HG)], sem.at[len(copies)]))
    for c in copies:
        c.start()
    for c in copies:
        c.wait()


def rims(x, g):
    any_spec = pl.BlockSpec(memory_space=pltpu.HBM)
    shape = jax.ShapeDtypeStruct((2 * (HX + HG), D), BF16)
    return pl.pallas_call(
        take_rims,
        out_shape=(shape, shape),
        in_specs=[any_spec] * 2,
        out_specs=(any_spec, any_spec),
        scratch_shapes=[pltpu.SemaphoreType.DMA((8,))],
        compiler_params=pltpu.CompilerParams(vmem_limit_bytes=1024 * 1024),
        cost_estimate=pl.CostEstimate(flops=0, bytes_accessed=30_000_000, transcendentals=0),
    )(x, g)


def write_copies(src, dst, sem):
    copies = [pltpu.make_async_copy(src, dst.at[i], sem.at[i]) for i in range(4)]
    for c in copies:
        c.start()
    for c in copies:
        c.wait()


def four_copies(part):
    any_spec = pl.BlockSpec(memory_space=pltpu.HBM)
    return pl.pallas_call(
        write_copies,
        out_shape=jax.ShapeDtypeStruct((4,) + part.shape, part.dtype),
        in_specs=[any_spec],
        out_specs=any_spec,
        scratch_shapes=[pltpu.SemaphoreType.DMA((4,))],
        compiler_params=pltpu.CompilerParams(vmem_limit_bytes=1024 * 1024),
        cost_estimate=pl.CostEstimate(flops=0, bytes_accessed=1_200_000, transcendentals=0),
    )(part)


def gather_weight(own, turn, tails, heads, params):
    theirs = lax.rem(turn + 2, 4)
    quarter = lax.dynamic_slice_in_dim(own, theirs * QUART, QUART, axis=1)
    near = lax.all_gather(own, ("x", "core"), axis=0, tiled=True)
    far = lax.ppermute(quarter, ("zh", "zl"), [(i, 15 - i) for i in range(16)])
    far = four_copies(far)
    hp = lax.ppermute(tails, ("y", "zl"), shift(32, 1))
    hn = lax.ppermute(heads, ("y", "zl"), shift(32, -1))
    far = lax.all_to_all(far, "x", 0, 0)
    far, hp, hn, params = lax.optimization_barrier((far, hp, hn, params))
    far = far.reshape(4 * SHARD, QUART)
    ya = [
        far,
        lax.ppermute(far, "y", shift(4, 1)),
        lax.ppermute(far, "zl", [(i, i ^ 1) for i in range(8)]),
        lax.ppermute(far, "y", shift(4, -1)),
    ]
    yb = [lax.ppermute(part, "core", shift(2, 1)) for part in ya]
    return hp, hn, params, [near] + ya + yb


def reduce_all(packed):
    plane = ("x", "core", "y")
    parts = lax.all_to_all(packed.reshape(32, PACK // 32, 128), plane, 0, 0)
    mine = jnp.sum(parts, axis=0)
    line = lax.all_to_all(jnp.broadcast_to(mine[None], (16,) + mine.shape), ("zh", "zl"), 0, 0)
    mine = jnp.sum(line, axis=0)
    whole = lax.all_to_all(jnp.broadcast_to(mine[None], (32,) + mine.shape), plane, 0, 0)
    whole = whole.reshape(PACK, 128)[: LT * SLOT].reshape(LT, SLOT, 128)
    whole = jnp.swapaxes(whole, 0, 1).reshape(SLOT, D)
    return whole[:TAPS], whole[TAPS], whole[TAPS + 1]


def on_device(frames, lengths, owner_map, norm_gain, norm_bias, proj_weight, dw_kernel, out_grad):
    idx = lax.axis_index
    x = frames.reshape(2 * BLK, D)
    dy = out_grad.reshape(2 * BLK, D)
    seq = idx("y") * 8 + idx("zl")
    position = jnp.mod(seq - owner_map[0, 0], 32)
    turn = lax.rem(idx("y") + 2 * lax.rem(idx("zl"), 2), 4)
    scalars = jnp.stack([position, lengths[0], idx("zh"), idx("core"), turn, position, position, position]).astype(jnp.int32)

    tails, heads = rims(x, dy)
    params = jnp.concatenate([dw_kernel, norm_gain[None], norm_bias[None]], axis=0)
    hp, hn, params, pieces = gather_weight(proj_weight, turn, tails, heads, params)
    act, ig, packed = run_fused(
        scalars, x, dy, hp, hn, params, pieces)
    kernel_grad, gain_grad, bias_grad = reduce_all(packed)
    return act.reshape(1, 2 * BLK, D), ig.reshape(1, 2 * BLK, D), kernel_grad, gain_grad, bias_grad


def solution(mesh):
    fine = Mesh(mesh.devices.reshape(2, 4, 2, 4, 8), ("zh", "x", "core", "y", "zl"))
    dp, seq = ("zh", "x", "core"), ("y", "zl")
    return jax.shard_map(
        on_device,
        mesh=fine,
        in_specs=(P(dp, seq, None), P(dp), P(dp, None), P(), P(), P(dp, None), P(), P(dp, seq, None)),
        out_specs=(P(dp, seq, None), P(dp, seq, None), P(), P(), P()),
        check_vma=False,
    )
```

```python
import jax
import jax.numpy as jnp
from jax import lax
from jax.experimental import pallas as pl
from jax.experimental.pallas import tpu as pltpu
from jax.sharding import Mesh, PartitionSpec as P

D = 1536
TAPS = 31
BLK = 128
HX = 32
EXT = BLK + 2 * HX
HG = 16
EXG = BLK + 2 * HG
SHARD = 96
HALF = 768
QUART = 768
LT = D // 128
PACK = 512
GAIN_ROW = 384
BIAS_ROW = 400
EPS = 1e-05
F32 = jnp.float32
BF16 = jnp.bfloat16


def sigmoid(v):
    return 0.5 * jnp.tanh(0.5 * v) + 0.5


def shift(count, by):
    return [(i, (i + by) % count) for i in range(count)]


def fused(sc, x_hbm, og_hbm, hp, hn, dw, near, ya0, ya1, ya2, ya3, yb0, yb1, yb2, yb3,
          act_ref, ig_ref, red_ref,
          xe, oge, w, nrm, std, inv, gbuf, abuf, sbuf, slp, kacc, gh, gn,
          xsem, wsem):
    pos, length = sc[0], sc[1]
    zh, ci, turn = sc[2], sc[3], sc[4]

    xcopies = []

    def go(src, dst, sem, bag):
        c = pltpu.make_async_copy(src, dst, sem)
        c.start()
        bag.append(c)

    for s in range(2):
        before = jnp.maximum(s - jnp.where(pos == 0, 1, 0), 0)
        after = jnp.minimum(s + jnp.where(pos == 31, 1, 0), 1)
        n = 6 * s
        go(x_hbm.at[pl.ds(s * BLK, BLK)], xe.at[pl.ds(s * EXT + HX, BLK)], xsem.at[n], xcopies)
        go(hp.at[pl.ds(pl.multiple_of(before * HX, HX), HX)], xe.at[pl.ds(s * EXT, HX)], xsem.at[n + 1], xcopies)
        go(hn.at[pl.ds(pl.multiple_of(after * HX, HX), HX)], xe.at[pl.ds(s * EXT + HX + BLK, HX)], xsem.at[n + 2], xcopies)
        go(og_hbm.at[pl.ds(s * BLK, BLK)], oge.at[pl.ds(s * EXG + HG, BLK)], xsem.at[n + 3], xcopies)
        go(hp.at[pl.ds(pl.multiple_of(2 * HX + before * HG, HG), HG)], oge.at[pl.ds(s * EXG, HG)], xsem.at[n + 4], xcopies)
        go(hn.at[pl.ds(pl.multiple_of(2 * HX + after * HG, HG), HG)], oge.at[pl.ds(s * EXG + HG + BLK, HG)], xsem.at[n + 5], xcopies)

    wcopies = []

    def row_of(z, x, c):
        return pl.multiple_of((z * 8 + x * 2 + c) * SHARD, SHARD)

    go(near, w.at[pl.ds(pl.multiple_of(zh * HALF, HALF), HALF)], wsem.at[32], wcopies)
    k = 0
    for d, (ra, rb) in enumerate(((ya0, yb0), (ya1, yb1), (ya2, yb2), (ya3, yb3))):
        col = pl.multiple_of(lax.rem(turn + 4 - d, 4) * QUART, QUART)
        for r in range(4):
            go(ra.at[pl.ds(r * SHARD, SHARD)], w.at[pl.ds(row_of(1 - zh, r, ci), SHARD), pl.ds(col, QUART)], wsem.at[k], wcopies)
            go(rb.at[pl.ds(r * SHARD, SHARD)], w.at[pl.ds(row_of(1 - zh, r, 1 - ci), SHARD), pl.ds(col, QUART)], wsem.at[k + 1], wcopies)
            k += 2

    red_ref[...] = jnp.zeros((PACK, 128), F32)
    for c in xcopies:
        c.wait()

    gain_row = dw[TAPS:TAPS + 1, :]
    bias_row = dw[TAPS + 1:TAPS + 2, :]

    def norm_step(i, carry):
        rows = pl.ds(pl.multiple_of(i * 128, 128), 128)
        v = xe[rows, :].astype(F32)
        mean = jnp.sum(v, axis=1, keepdims=True) * (1.0 / D)
        c = v - mean
        var = jnp.sum(c * c, axis=1, keepdims=True) * (1.0 / D)
        iv = lax.rsqrt(var + EPS)
        st = c * iv
        std[rows, :] = st
        inv[rows, :] = jnp.broadcast_to(iv, (128, 128))
        nrm[rows, :] = (st * gain_row + bias_row).astype(BF16)
        return carry

    lax.fori_loop(0, 2 * EXT // 128, norm_step, 0)

    for c in wcopies:
        c.wait()

    row384 = lax.broadcasted_iota(jnp.int32, (2 * EXT, 128), 0)
    second = row384 >= EXT
    t384 = pos * BLK + jnp.where(second, row384 - EXT + 32 * BLK, row384) - HX
    live384 = (t384 >= 0) & (t384 < length)
    iota16 = lax.broadcasted_iota(jnp.int32, (16, 128), 0)

    def chan_step(j, carry):
        col = pl.multiple_of(j * 256, 256)
        normed = nrm[...]
        a = jnp.dot(normed, w[:, pl.ds(col, 256)], preferred_element_type=F32)
        b = jnp.dot(normed, w[:, pl.ds(D + col, 256)], preferred_element_type=F32)
        sg = sigmoid(b)
        for h in range(2):
            ah = a[:, h * 128:(h + 1) * 128]
            sh = sg[:, h * 128:(h + 1) * 128]
            abuf[h] = ah
            sbuf[h] = sh
            gbuf[h] = jnp.where(live384, ah * sh, 0.0).astype(BF16).astype(F32)

        def tile_step(q, carry2):
            h = q // 2
            s = q % 2
            lane = pl.multiple_of((2 * j + h) * 128, 128)
            first = (pos + 32 * s) * BLK
            ext0 = s * EXT

            @pl.when(s == 0)
            def _():
                for k in range(TAPS):
                    kacc[k] = jnp.zeros((8, 128), F32)

            taps = [jnp.broadcast_to(dw[k:k + 1, pl.ds(lane, 128)], (8, 128)) for k in range(TAPS)]
            acc = {}
            done = {}
            for o in range(1, 8 * 19 + 32):
                v = gbuf[h, pl.ds(ext0 + o, 8), :]
                for i in range(20):
                    k = o - 1 - 8 * i
                    if 0 <= k < TAPS:
                        p = v * taps[k]
                        acc[i] = p if k == 0 else acc[i] + p
                        if k == TAPS - 1:
                            done[i] = acc.pop(i)
                            if i % 2 == 1:
                                m = i // 2
                                conv = jnp.concatenate([done.pop(i - 1), done.pop(i)], axis=0)
                                cs = sigmoid(conv)
                                t = iota16 + (first + 16 * m - HG)
                                live = (t >= 0) & (t < length)
                                og = oge[pl.ds(pl.multiple_of(s * EXG + 16 * m, 16), 16), pl.ds(lane, 128)].astype(F32)
                                av = conv * cs
                                sl = jnp.where(live, og * (cs + av * (1.0 - cs)), 0.0).astype(BF16).astype(F32)
                                slp[pl.ds(16 * m, 16), :] = sl
                                if 1 <= m <= 8:
                                    act_ref[pl.ds(pl.multiple_of(s * BLK + 16 * (m - 1), 16), 16), pl.ds(lane, 128)] = (
                                        jnp.where(live, av, 0.0).astype(BF16))

            ks = [kacc[k] for k in range(TAPS)]
            sv = {}
            for o in range(17, 17 + 8 * 15 + TAPS):
                v = gbuf[h, pl.ds(ext0 + o, 8), :]
                for i in range(16):
                    k = o - 17 - 8 * i
                    if 0 <= k < TAPS:
                        if k == 0:
                            sv[i] = slp[pl.ds(16 + 8 * i, 8), :]
                        ks[k] = ks[k] + v * sv[i]
            for k in range(TAPS):
                kacc[k] = ks[k]

            @pl.when(s == 1)
            def _():
                for k in range(TAPS):
                    red_ref[pl.ds((k // 8) * 8 * LT + k % 8 + (2 * j + h) * 8, 1), :] = jnp.sum(ks[k], axis=0, keepdims=True)

            acc = {}
            done = {}
            for o in range(1, 8 * 15 + 32):
                v = slp[pl.ds(o, 8), :]
                for i in range(16):
                    k = 31 + 8 * i - o
                    if 0 <= k < TAPS:
                        p = v * taps[k]
                        acc[i] = p if k == TAPS - 1 else acc[i] + p
                        if k == 0:
                            done[i] = acc.pop(i)
                            if i % 2 == 1:
                                m = i // 2
                                back = jnp.concatenate([done.pop(i - 1), done.pop(i)], axis=0)
                                t = iota16 + (first + 16 * m)
                                back = jnp.where(t < length, back, 0.0)
                                rows = pl.ds(pl.multiple_of(ext0 + HX + 16 * m, 16), 16)
                                av = abuf[h, rows, :]
                                sgv = sbuf[h, rows, :]
                                ga = back * sgv
                                out = pl.ds(pl.multiple_of(s * BLK + 16 * m, 16), 16)
                                gh[out, pl.ds(lane, 128)] = ga.astype(BF16)
                                gh[out, pl.ds(D + lane, 128)] = (ga * av * (1.0 - sgv)).astype(BF16)
            return carry2

        lax.fori_loop(0, 4, tile_step, 0)
        return carry

    lax.fori_loop(0, D // 256, chan_step, 0)

    gn[...] = lax.dot_general(gh[...], w[...], (((1,), (1,)), ((), ())), preferred_element_type=F32)

    def grad_step(i, carry):
        gsum, bsum = carry
        src = pl.ds(pl.multiple_of(jnp.where(i >= 2, EXT - BLK, 0) + HX + i * 64, 32), 64)
        dst = pl.ds(pl.multiple_of(i * 64, 64), 64)
        g = gn[dst, :]
        st = std[src, :]
        gs = g * st
        for q in range(8):
            gsum = gsum + gs[q * 8:(q + 1) * 8]
            bsum = bsum + g[q * 8:(q + 1) * 8]
        sc_ = g * gain_row
        m1 = jnp.sum(sc_, axis=1, keepdims=True) * (1.0 / D)
        m2 = jnp.sum(sc_ * st, axis=1, keepdims=True) * (1.0 / D)
        iv = inv[src, 0:1]
        ig_ref[dst, :] = (iv * (sc_ - m1 - st * m2)).astype(BF16)
        return gsum, bsum

    zero = jnp.zeros((8, D), F32)
    gsum, bsum = lax.fori_loop(0, 4, grad_step, (zero, zero))
    grow = jnp.sum(gsum, axis=0, keepdims=True)
    brow = jnp.sum(bsum, axis=0, keepdims=True)
    for l in range(LT):
        red_ref[GAIN_ROW + l:GAIN_ROW + l + 1, :] = grow[:, l * 128:(l + 1) * 128]
        red_ref[BIAS_ROW + l:BIAS_ROW + l + 1, :] = brow[:, l * 128:(l + 1) * 128]


def run_fused(scalars, frames, out_grad, hp, hn, params, pieces):
    any_spec = pl.BlockSpec(memory_space=pltpu.HBM)
    vm = pl.BlockSpec(memory_space=pltpu.VMEM)
    return pl.pallas_call(
        fused,
        out_shape=(
            jax.ShapeDtypeStruct((2 * BLK, D), BF16),
            jax.ShapeDtypeStruct((2 * BLK, D), BF16),
            jax.ShapeDtypeStruct((PACK, 128), F32),
        ),
        in_specs=[pl.BlockSpec(memory_space=pltpu.SMEM)] + [any_spec] * 4 + [vm] + [any_spec] * len(pieces),
        out_specs=(vm, vm, vm),
        scratch_shapes=[
            pltpu.VMEM((2 * EXT, D), BF16),
            pltpu.VMEM((2 * EXG, D), BF16),
            pltpu.VMEM((D, 2 * D), BF16),
            pltpu.VMEM((2 * EXT, D), BF16),
            pltpu.VMEM((2 * EXT, D), F32),
            pltpu.VMEM((2 * EXT, 128), F32),
            pltpu.VMEM((2, 2 * EXT, 128), F32),
            pltpu.VMEM((2, 2 * EXT, 128), F32),
            pltpu.VMEM((2, 2 * EXT, 128), F32),
            pltpu.VMEM((EXG, 128), F32),
            pltpu.VMEM((TAPS, 8, 128), F32),
            pltpu.VMEM((2 * BLK, 2 * D), BF16),
            pltpu.VMEM((2 * BLK, D), F32),
            pltpu.SemaphoreType.DMA((12,)),
            pltpu.SemaphoreType.DMA((40,)),
        ],
        compiler_params=pltpu.CompilerParams(vmem_limit_bytes=48 * 1024 * 1024),
        cost_estimate=pl.CostEstimate(flops=9_000_000_000, bytes_accessed=14_000_000, transcendentals=2_000_000),
    )(scalars, frames, out_grad, hp, hn, params, *pieces)


def take_rims(x, g, tails, heads, sem):
    copies = []
    for dst, fx, fg in ((tails, BLK - HX, BLK - HG), (heads, 0, 0)):
        for s in range(2):
            copies.append(pltpu.make_async_copy(x.at[pl.ds(s * BLK + fx, HX)], dst.at[pl.ds(s * HX, HX)], sem.at[len(copies)]))
            copies.append(pltpu.make_async_copy(g.at[pl.ds(s * BLK + fg, HG)], dst.at[pl.ds(2 * HX + s * HG, HG)], sem.at[len(copies)]))
    for c in copies:
        c.start()
    for c in copies:
        c.wait()


def rims(x, g):
    any_spec = pl.BlockSpec(memory_space=pltpu.HBM)
    shape = jax.ShapeDtypeStruct((2 * (HX + HG), D), BF16)
    return pl.pallas_call(
        take_rims,
        out_shape=(shape, shape),
        in_specs=[any_spec] * 2,
        out_specs=(any_spec, any_spec),
        scratch_shapes=[pltpu.SemaphoreType.DMA((8,))],
        compiler_params=pltpu.CompilerParams(vmem_limit_bytes=1024 * 1024),
        cost_estimate=pl.CostEstimate(flops=0, bytes_accessed=30_000_000, transcendentals=0),
    )(x, g)


def write_copies(src, dst, sem):
    copies = [pltpu.make_async_copy(src, dst.at[i], sem.at[i]) for i in range(4)]
    for c in copies:
        c.start()
    for c in copies:
        c.wait()


def four_copies(part):
    any_spec = pl.BlockSpec(memory_space=pltpu.HBM)
    return pl.pallas_call(
        write_copies,
        out_shape=jax.ShapeDtypeStruct((4,) + part.shape, part.dtype),
        in_specs=[any_spec],
        out_specs=any_spec,
        scratch_shapes=[pltpu.SemaphoreType.DMA((4,))],
        compiler_params=pltpu.CompilerParams(vmem_limit_bytes=1024 * 1024),
        cost_estimate=pl.CostEstimate(flops=0, bytes_accessed=1_200_000, transcendentals=0),
    )(part)


def gather_weight(own, turn, tails, heads, params):
    theirs = lax.rem(turn + 2, 4)
    quarter = lax.dynamic_slice_in_dim(own, theirs * QUART, QUART, axis=1)
    near = lax.all_gather(own, ("x", "core"), axis=0, tiled=True)
    far = lax.ppermute(quarter, ("zh", "zl"), [(i, 15 - i) for i in range(16)])
    far = four_copies(far)
    far, tails, heads, params = lax.optimization_barrier((far, tails, heads, params))
    hp = lax.ppermute(tails, ("y", "zl"), shift(32, 1))
    hn = lax.ppermute(heads, ("y", "zl"), shift(32, -1))
    far = lax.all_to_all(far, "x", 0, 0)
    far, hp, hn = lax.optimization_barrier((far, hp, hn))
    far = far.reshape(4 * SHARD, QUART)
    ya = [
        far,
        lax.ppermute(far, "y", shift(4, 1)),
        lax.ppermute(far, "zl", [(i, i ^ 1) for i in range(8)]),
        lax.ppermute(far, "y", shift(4, -1)),
    ]
    yb = [lax.ppermute(part, "core", shift(2, 1)) for part in ya]
    return hp, hn, params, [near] + ya + yb


def reduce_all(packed):
    plane = ("x", "core", "y")
    parts = lax.all_to_all(packed.reshape(32, PACK // 32, 128), plane, 0, 0)
    mine = jnp.sum(parts, axis=0)
    line = lax.all_to_all(jnp.broadcast_to(mine[None], (16,) + mine.shape), ("zh", "zl"), 0, 0)
    mine = jnp.sum(line, axis=0)
    whole = lax.all_to_all(jnp.broadcast_to(mine[None], (32,) + mine.shape), plane, 0, 0)
    whole = whole.reshape(PACK, 128)
    taps = whole[:GAIN_ROW].reshape(4, LT, 8, 128).transpose(0, 2, 1, 3).reshape(32, D)[:TAPS]
    return taps, whole[GAIN_ROW:GAIN_ROW + LT].reshape(D), whole[BIAS_ROW:BIAS_ROW + LT].reshape(D)


def on_device(frames, lengths, owner_map, norm_gain, norm_bias, proj_weight, dw_kernel, out_grad):
    idx = lax.axis_index
    x = frames.reshape(2 * BLK, D)
    dy = out_grad.reshape(2 * BLK, D)
    seq = idx("y") * 8 + idx("zl")
    position = jnp.mod(seq - owner_map[0, 0], 32)
    turn = lax.rem(idx("y") + 2 * lax.rem(idx("zl"), 2), 4)
    scalars = jnp.stack([position, lengths[0], idx("zh"), idx("core"), turn, position, position, position]).astype(jnp.int32)

    tails, heads = rims(x, dy)
    params = jnp.concatenate([dw_kernel, norm_gain[None], norm_bias[None]], axis=0)
    hp, hn, params, pieces = gather_weight(proj_weight, turn, tails, heads, params)
    act, ig, packed = run_fused(
        scalars, x, dy, hp, hn, params, pieces)
    kernel_grad, gain_grad, bias_grad = reduce_all(packed)
    return act.reshape(1, 2 * BLK, D), ig.reshape(1, 2 * BLK, D), kernel_grad, gain_grad, bias_grad


def solution(mesh):
    fine = Mesh(mesh.devices.reshape(2, 4, 2, 4, 8), ("zh", "x", "core", "y", "zl"))
    dp, seq = ("zh", "x", "core"), ("y", "zl")
    return jax.shard_map(
        on_device,
        mesh=fine,
        in_specs=(P(dp, seq, None), P(dp), P(dp, None), P(), P(), P(dp, None), P(), P(dp, seq, None)),
        out_specs=(P(dp, seq, None), P(dp, seq, None), P(), P(), P()),
        check_vma=False,
    )
```

```python
import jax
import jax.numpy as jnp
from jax import lax
from jax.experimental import pallas as pl
from jax.experimental.pallas import tpu as pltpu
from jax.sharding import Mesh, PartitionSpec as P

D = 1536
TAPS = 31
BLK = 128
HX = 32
EXT = BLK + 2 * HX
HG = 16
EXG = BLK + 2 * HG
RIM = HX + HG
SHARD = 96
HALF = 768
QUART = 768
LT = D // 128
PACK = 512
GAIN_ROW = 384
BIAS_ROW = 400
EPS = 1e-05
F32 = jnp.float32
BF16 = jnp.bfloat16


def sigmoid(v):
    return 0.5 * jnp.tanh(0.5 * v) + 0.5


def shift(count, by):
    return [(i, (i + by) % count) for i in range(count)]


def fused(sc, x_hbm, og_hbm, rim_a, rim_b, dw, near, ya0, ya1, ya2, ya3, yb0, yb1, yb2, yb3,
          act_ref, ig_ref, red_ref,
          xe, oge, w, nrm, std, inv, gbuf, abuf, sbuf, slp, kacc, gh, gn,
          xsem, wsem):
    pos, length = sc[0], sc[1]
    zh, ci, turn = sc[2], sc[3], sc[4]

    xcopies = []

    def go(src, dst, sem, bag):
        c = pltpu.make_async_copy(src, dst, sem)
        c.start()
        bag.append(c)

    even = sc[5] == 0

    def pick(when_even, when_odd, rows, dst, sem):
        @pl.when(even)
        def _():
            pltpu.make_async_copy(when_even.at[rows], dst, sem).start()

        @pl.when(jnp.logical_not(even))
        def _():
            pltpu.make_async_copy(when_odd.at[rows], dst, sem).start()

        xcopies.append(pltpu.make_async_copy(when_odd.at[rows], dst, sem))

    for s in range(2):
        before = jnp.maximum(s - jnp.where(pos == 0, 1, 0), 0)
        after = jnp.minimum(s + jnp.where(pos == 31, 1, 0), 1)
        hp = pl.multiple_of(before * RIM, 16)
        hn = pl.multiple_of(after * RIM, 16)
        n = 6 * s
        go(x_hbm.at[pl.ds(s * BLK, BLK)], xe.at[pl.ds(s * EXT + HX, BLK)], xsem.at[n], xcopies)
        pick(rim_b, rim_a, pl.ds(hp, HX), xe.at[pl.ds(s * EXT, HX)], xsem.at[n + 1])
        pick(rim_a, rim_b, pl.ds(hn, HX), xe.at[pl.ds(s * EXT + HX + BLK, HX)], xsem.at[n + 2])
        go(og_hbm.at[pl.ds(s * BLK, BLK)], oge.at[pl.ds(s * EXG + HG, BLK)], xsem.at[n + 3], xcopies)
        pick(rim_b, rim_a, pl.ds(hp + HX, HG), oge.at[pl.ds(s * EXG, HG)], xsem.at[n + 4])
        pick(rim_a, rim_b, pl.ds(hn + HX, HG), oge.at[pl.ds(s * EXG + HG + BLK, HG)], xsem.at[n + 5])

    wcopies = []

    def row_of(z, x, c):
        return pl.multiple_of((z * 8 + x * 2 + c) * SHARD, SHARD)

    go(near, w.at[pl.ds(pl.multiple_of(zh * HALF, HALF), HALF)], wsem.at[32], wcopies)
    k = 0
    for d, (ra, rb) in enumerate(((ya0, yb0), (ya1, yb1), (ya2, yb2), (ya3, yb3))):
        col = pl.multiple_of(lax.rem(turn + 4 - d, 4) * QUART, QUART)
        for r in range(4):
            go(ra.at[pl.ds(r * SHARD, SHARD)], w.at[pl.ds(row_of(1 - zh, r, ci), SHARD), pl.ds(col, QUART)], wsem.at[k], wcopies)
            go(rb.at[pl.ds(r * SHARD, SHARD)], w.at[pl.ds(row_of(1 - zh, r, 1 - ci), SHARD), pl.ds(col, QUART)], wsem.at[k + 1], wcopies)
            k += 2

    red_ref[...] = jnp.zeros((PACK, 128), F32)
    for c in xcopies:
        c.wait()

    gain_row = dw[TAPS:TAPS + 1, :]
    bias_row = dw[TAPS + 1:TAPS + 2, :]

    def norm_step(i, carry):
        rows = pl.ds(pl.multiple_of(i * 128, 128), 128)
        v = xe[rows, :].astype(F32)
        mean = jnp.sum(v, axis=1, keepdims=True) * (1.0 / D)
        c = v - mean
        var = jnp.sum(c * c, axis=1, keepdims=True) * (1.0 / D)
        iv = lax.rsqrt(var + EPS)
        st = c * iv
        std[rows, :] = st
        inv[rows, :] = jnp.broadcast_to(iv, (128, 128))
        nrm[rows, :] = (st * gain_row + bias_row).astype(BF16)
        return carry

    lax.fori_loop(0, 2 * EXT // 128, norm_step, 0)

    for c in wcopies:
        c.wait()

    row384 = lax.broadcasted_iota(jnp.int32, (2 * EXT, 128), 0)
    second = row384 >= EXT
    t384 = pos * BLK + jnp.where(second, row384 - EXT + 32 * BLK, row384) - HX
    live384 = (t384 >= 0) & (t384 < length)
    iota16 = lax.broadcasted_iota(jnp.int32, (16, 128), 0)

    def chan_step(j, carry):
        col = pl.multiple_of(j * 256, 256)
        normed = nrm[...]
        a = jnp.dot(normed, w[:, pl.ds(col, 256)], preferred_element_type=F32)
        b = jnp.dot(normed, w[:, pl.ds(D + col, 256)], preferred_element_type=F32)
        sg = sigmoid(b)
        for h in range(2):
            ah = a[:, h * 128:(h + 1) * 128]
            sh = sg[:, h * 128:(h + 1) * 128]
            abuf[h] = ah
            sbuf[h] = sh
            gbuf[h] = jnp.where(live384, ah * sh, 0.0).astype(BF16).astype(F32)

        def tile_step(q, carry2):
            h = q // 2
            s = q % 2
            lane = pl.multiple_of((2 * j + h) * 128, 128)
            first = (pos + 32 * s) * BLK
            ext0 = s * EXT

            @pl.when(s == 0)
            def _():
                for k in range(TAPS):
                    kacc[k] = jnp.zeros((8, 128), F32)

            taps = [jnp.broadcast_to(dw[k:k + 1, pl.ds(lane, 128)], (8, 128)) for k in range(TAPS)]
            acc = {}
            done = {}
            for o in range(1, 8 * 19 + 32):
                v = gbuf[h, pl.ds(ext0 + o, 8), :]
                for i in range(20):
                    k = o - 1 - 8 * i
                    if 0 <= k < TAPS:
                        p = v * taps[k]
                        acc[i] = p if k == 0 else acc[i] + p
                        if k == TAPS - 1:
                            done[i] = acc.pop(i)
                            if i % 2 == 1:
                                m = i // 2
                                conv = jnp.concatenate([done.pop(i - 1), done.pop(i)], axis=0)
                                cs = sigmoid(conv)
                                t = iota16 + (first + 16 * m - HG)
                                live = (t >= 0) & (t < length)
                                og = oge[pl.ds(pl.multiple_of(s * EXG + 16 * m, 16), 16), pl.ds(lane, 128)].astype(F32)
                                av = conv * cs
                                sl = jnp.where(live, og * (cs + av * (1.0 - cs)), 0.0).astype(BF16).astype(F32)
                                slp[pl.ds(16 * m, 16), :] = sl
                                if 1 <= m <= 8:
                                    act_ref[pl.ds(pl.multiple_of(s * BLK + 16 * (m - 1), 16), 16), pl.ds(lane, 128)] = (
                                        jnp.where(live, av, 0.0).astype(BF16))

            ks = [kacc[k] for k in range(TAPS)]
            sv = {}
            for o in range(17, 17 + 8 * 15 + TAPS):
                v = gbuf[h, pl.ds(ext0 + o, 8), :]
                for i in range(16):
                    k = o - 17 - 8 * i
                    if 0 <= k < TAPS:
                        if k == 0:
                            sv[i] = slp[pl.ds(16 + 8 * i, 8), :]
                        ks[k] = ks[k] + v * sv[i]
            for k in range(TAPS):
                kacc[k] = ks[k]

            @pl.when(s == 1)
            def _():
                for k in range(TAPS):
                    red_ref[pl.ds((k // 8) * 8 * LT + k % 8 + (2 * j + h) * 8, 1), :] = jnp.sum(ks[k], axis=0, keepdims=True)

            acc = {}
            done = {}
            for o in range(1, 8 * 15 + 32):
                v = slp[pl.ds(o, 8), :]
                for i in range(16):
                    k = 31 + 8 * i - o
                    if 0 <= k < TAPS:
                        p = v * taps[k]
                        acc[i] = p if k == TAPS - 1 else acc[i] + p
                        if k == 0:
                            done[i] = acc.pop(i)
                            if i % 2 == 1:
                                m = i // 2
                                back = jnp.concatenate([done.pop(i - 1), done.pop(i)], axis=0)
                                t = iota16 + (first + 16 * m)
                                back = jnp.where(t < length, back, 0.0)
                                rows = pl.ds(pl.multiple_of(ext0 + HX + 16 * m, 16), 16)
                                av = abuf[h, rows, :]
                                sgv = sbuf[h, rows, :]
                                ga = back * sgv
                                out = pl.ds(pl.multiple_of(s * BLK + 16 * m, 16), 16)
                                gh[out, pl.ds(lane, 128)] = ga.astype(BF16)
                                gh[out, pl.ds(D + lane, 128)] = (ga * av * (1.0 - sgv)).astype(BF16)
            return carry2

        lax.fori_loop(0, 4, tile_step, 0)
        return carry

    lax.fori_loop(0, D // 256, chan_step, 0)

    gn[...] = lax.dot_general(gh[...], w[...], (((1,), (1,)), ((), ())), preferred_element_type=F32)

    def grad_step(i, carry):
        gsum, bsum = carry
        src = pl.ds(pl.multiple_of(jnp.where(i >= 2, EXT - BLK, 0) + HX + i * 64, 32), 64)
        dst = pl.ds(pl.multiple_of(i * 64, 64), 64)
        g = gn[dst, :]
        st = std[src, :]
        gs = g * st
        for q in range(8):
            gsum = gsum + gs[q * 8:(q + 1) * 8]
            bsum = bsum + g[q * 8:(q + 1) * 8]
        sc_ = g * gain_row
        m1 = jnp.sum(sc_, axis=1, keepdims=True) * (1.0 / D)
        m2 = jnp.sum(sc_ * st, axis=1, keepdims=True) * (1.0 / D)
        iv = inv[src, 0:1]
        ig_ref[dst, :] = (iv * (sc_ - m1 - st * m2)).astype(BF16)
        return gsum, bsum

    zero = jnp.zeros((8, D), F32)
    gsum, bsum = lax.fori_loop(0, 4, grad_step, (zero, zero))
    grow = jnp.sum(gsum, axis=0, keepdims=True)
    brow = jnp.sum(bsum, axis=0, keepdims=True)
    for l in range(LT):
        red_ref[GAIN_ROW + l:GAIN_ROW + l + 1, :] = grow[:, l * 128:(l + 1) * 128]
        red_ref[BIAS_ROW + l:BIAS_ROW + l + 1, :] = brow[:, l * 128:(l + 1) * 128]


def run_fused(scalars, frames, out_grad, rim_a, rim_b, params, pieces):
    any_spec = pl.BlockSpec(memory_space=pltpu.HBM)
    vm = pl.BlockSpec(memory_space=pltpu.VMEM)
    return pl.pallas_call(
        fused,
        out_shape=(
            jax.ShapeDtypeStruct((2 * BLK, D), BF16),
            jax.ShapeDtypeStruct((2 * BLK, D), BF16),
            jax.ShapeDtypeStruct((PACK, 128), F32),
        ),
        in_specs=[pl.BlockSpec(memory_space=pltpu.SMEM)] + [any_spec] * 4 + [vm] + [any_spec] * len(pieces),
        out_specs=(vm, vm, vm),
        scratch_shapes=[
            pltpu.VMEM((2 * EXT, D), BF16),
            pltpu.VMEM((2 * EXG, D), BF16),
            pltpu.VMEM((D, 2 * D), BF16),
            pltpu.VMEM((2 * EXT, D), BF16),
            pltpu.VMEM((2 * EXT, D), F32),
            pltpu.VMEM((2 * EXT, 128), F32),
            pltpu.VMEM((2, 2 * EXT, 128), F32),
            pltpu.VMEM((2, 2 * EXT, 128), F32),
            pltpu.VMEM((2, 2 * EXT, 128), F32),
            pltpu.VMEM((EXG, 128), F32),
            pltpu.VMEM((TAPS, 8, 128), F32),
            pltpu.VMEM((2 * BLK, 2 * D), BF16),
            pltpu.VMEM((2 * BLK, D), F32),
            pltpu.SemaphoreType.DMA((12,)),
            pltpu.SemaphoreType.DMA((40,)),
        ],
        compiler_params=pltpu.CompilerParams(vmem_limit_bytes=51 * 1024 * 1024),
        cost_estimate=pl.CostEstimate(flops=9_000_000_000, bytes_accessed=14_000_000, transcendentals=2_000_000),
    )(scalars, frames, out_grad, rim_a, rim_b, params, *pieces)


def take_rims(sc, x, g, near, far, sem):
    even = sc[5] == 0
    copies = []

    def go(src, dst):
        copies.append(pltpu.make_async_copy(src, dst, sem.at[len(copies)]))
        copies[-1].start()

    for s in range(2):
        last = s * BLK + BLK
        for dst, tail in ((near, even), (far, jnp.logical_not(even))):
            fx = pl.multiple_of(jnp.where(tail, last - HX, s * BLK), 16)
            fg = pl.multiple_of(jnp.where(tail, last - HG, s * BLK), 16)
            go(x.at[pl.ds(fx, HX)], dst.at[pl.ds(s * RIM, HX)])
            go(g.at[pl.ds(fg, HG)], dst.at[pl.ds(s * RIM + HX, HG)])
    for c in copies:
        c.wait()


def rims(scalars, x, g):
    any_spec = pl.BlockSpec(memory_space=pl.ANY)
    both = jax.ShapeDtypeStruct((2 * RIM, D), BF16)
    return pl.pallas_call(
        take_rims,
        out_shape=(both, both),
        in_specs=[pl.BlockSpec(memory_space=pltpu.SMEM), any_spec, any_spec],
        out_specs=(any_spec, any_spec),
        scratch_shapes=[pltpu.SemaphoreType.DMA((8,))],
        compiler_params=pltpu.CompilerParams(vmem_limit_bytes=1024 * 1024),
        cost_estimate=pl.CostEstimate(flops=0, bytes_accessed=1_200_000, transcendentals=0),
    )(scalars, x, g)


def write_copies(src, dst, sem):
    copies = [pltpu.make_async_copy(src, dst.at[i], sem.at[i]) for i in range(4)]
    for c in copies:
        c.start()
    for c in copies:
        c.wait()


def four_copies(part):
    any_spec = pl.BlockSpec(memory_space=pltpu.HBM)
    return pl.pallas_call(
        write_copies,
        out_shape=jax.ShapeDtypeStruct((4,) + part.shape, part.dtype),
        in_specs=[any_spec],
        out_specs=any_spec,
        scratch_shapes=[pltpu.SemaphoreType.DMA((4,))],
        compiler_params=pltpu.CompilerParams(vmem_limit_bytes=1024 * 1024),
        cost_estimate=pl.CostEstimate(flops=0, bytes_accessed=1_200_000, transcendentals=0),
    )(part)


def meet_next():
    pairs = []
    for i in range(1, 32, 2):
        pairs += [(i, (i + 1) % 32), ((i + 1) % 32, i)]
    return pairs


def gather_weight(own, turn, rim_a, rim_b, params):
    theirs = lax.rem(turn + 2, 4)
    quarter = lax.dynamic_slice_in_dim(own, theirs * QUART, QUART, axis=1)
    near = lax.all_gather(own, ("x", "core"), axis=0, tiled=True)
    far = lax.ppermute(quarter, ("zh", "zl"), [(i, 15 - i) for i in range(16)])
    far = four_copies(far)
    far, rim_a, rim_b, params = lax.optimization_barrier((far, rim_a, rim_b, params))
    a = lax.ppermute(rim_a, ("y", "zl"), [(i, i ^ 1) for i in range(32)])
    b = lax.ppermute(rim_b, ("y", "zl"), meet_next())
    far = lax.all_to_all(far, "x", 0, 0)
    far, a, b = lax.optimization_barrier((far, a, b))
    far = far.reshape(4 * SHARD, QUART)
    ya = [
        far,
        lax.ppermute(far, "y", shift(4, 1)),
        lax.ppermute(far, "zl", [(i, i ^ 1) for i in range(8)]),
        lax.ppermute(far, "y", shift(4, -1)),
    ]
    yb = [lax.ppermute(part, "core", shift(2, 1)) for part in ya]
    return a, b, params, [near] + ya + yb


def reduce_all(packed):
    plane = ("x", "core", "y")
    parts = lax.all_to_all(packed.reshape(32, PACK // 32, 128), plane, 0, 0)
    mine = jnp.sum(parts, axis=0)
    line = lax.all_to_all(jnp.broadcast_to(mine[None], (16,) + mine.shape), ("zh", "zl"), 0, 0)
    mine = jnp.sum(line, axis=0)
    whole = lax.all_to_all(jnp.broadcast_to(mine[None], (32,) + mine.shape), plane, 0, 0)
    whole = whole.reshape(PACK, 128)
    taps = whole[:GAIN_ROW].reshape(4, LT, 8, 128).transpose(0, 2, 1, 3).reshape(32, D)[:TAPS]
    return taps, whole[GAIN_ROW:GAIN_ROW + LT].reshape(D), whole[BIAS_ROW:BIAS_ROW + LT].reshape(D)


def on_device(frames, lengths, owner_map, norm_gain, norm_bias, proj_weight, dw_kernel, out_grad):
    idx = lax.axis_index
    x = frames.reshape(2 * BLK, D)
    dy = out_grad.reshape(2 * BLK, D)
    seq = idx("y") * 8 + idx("zl")
    position = jnp.mod(seq - owner_map[0, 0], 32)
    turn = lax.rem(idx("y") + 2 * lax.rem(idx("zl"), 2), 4)
    scalars = jnp.stack([position, lengths[0], idx("zh"), idx("core"), turn, lax.rem(idx("zl"), 2), position, position]).astype(jnp.int32)

    rim_a, rim_b = rims(scalars, x, dy)
    params = jnp.concatenate([dw_kernel, norm_gain[None], norm_bias[None]], axis=0)
    rim_a, rim_b, params, pieces = gather_weight(proj_weight, turn, rim_a, rim_b, params)
    act, ig, packed = run_fused(
        scalars, x, dy, rim_a, rim_b, params, pieces)
    kernel_grad, gain_grad, bias_grad = reduce_all(packed)
    return act.reshape(1, 2 * BLK, D), ig.reshape(1, 2 * BLK, D), kernel_grad, gain_grad, bias_grad


def solution(mesh):
    fine = Mesh(mesh.devices.reshape(2, 4, 2, 4, 8), ("zh", "x", "core", "y", "zl"))
    dp, seq = ("zh", "x", "core"), ("y", "zl")
    return jax.shard_map(
        on_device,
        mesh=fine,
        in_specs=(P(dp, seq, None), P(dp), P(dp, None), P(), P(), P(dp, None), P(), P(dp, seq, None)),
        out_specs=(P(dp, seq, None), P(dp, seq, None), P(), P(), P()),
        check_vma=False,
    )
```

```python
import jax
import jax.numpy as jnp
from jax import lax
from jax.experimental import pallas as pl
from jax.experimental.pallas import tpu as pltpu
from jax.sharding import Mesh, PartitionSpec as P

D = 1536
TAPS = 31
BLK = 128
HX = 32
EXT = BLK + 2 * HX
HG = 16
EXG = BLK + 2 * HG
RIM = HX + HG
SHARD = 96
HALF = 768
QUART = 768
LT = D // 128
PACK = 512
GAIN_ROW = 384
BIAS_ROW = 400
EPS = 1e-05
F32 = jnp.float32
BF16 = jnp.bfloat16


def sigmoid(v):
    return 0.5 * jnp.tanh(0.5 * v) + 0.5


def shift(count, by):
    return [(i, (i + by) % count) for i in range(count)]


def fused(sc, x_hbm, og_hbm, rim_a, rim_b, dw, near, ya0, ya1, ya2, ya3, yb0, yb1, yb2, yb3,
          act_hbm, ig_ref, red_ref,
          act_ref, xe, oge, w, nrm, std, inv, gbuf, abuf, sbuf, slp, kacc, gh, gn,
          xsem, wsem):
    pos, length = sc[0], sc[1]
    zh, ci, turn = sc[2], sc[3], sc[4]

    xcopies = []

    def go(src, dst, sem, bag):
        c = pltpu.make_async_copy(src, dst, sem)
        c.start()
        bag.append(c)

    even = sc[5] == 0

    def pick(when_even, when_odd, rows, dst, sem):
        @pl.when(even)
        def _():
            pltpu.make_async_copy(when_even.at[rows], dst, sem).start()

        @pl.when(jnp.logical_not(even))
        def _():
            pltpu.make_async_copy(when_odd.at[rows], dst, sem).start()

        xcopies.append(pltpu.make_async_copy(when_odd.at[rows], dst, sem))

    for s in range(2):
        before = jnp.maximum(s - jnp.where(pos == 0, 1, 0), 0)
        after = jnp.minimum(s + jnp.where(pos == 31, 1, 0), 1)
        hp = pl.multiple_of(before * RIM, 16)
        hn = pl.multiple_of(after * RIM, 16)
        n = 6 * s
        go(x_hbm.at[pl.ds(s * BLK, BLK)], xe.at[pl.ds(s * EXT + HX, BLK)], xsem.at[n], xcopies)
        pick(rim_b, rim_a, pl.ds(hp, HX), xe.at[pl.ds(s * EXT, HX)], xsem.at[n + 1])
        pick(rim_a, rim_b, pl.ds(hn, HX), xe.at[pl.ds(s * EXT + HX + BLK, HX)], xsem.at[n + 2])
        go(og_hbm.at[pl.ds(s * BLK, BLK)], oge.at[pl.ds(s * EXG + HG, BLK)], xsem.at[n + 3], xcopies)
        pick(rim_b, rim_a, pl.ds(hp + HX, HG), oge.at[pl.ds(s * EXG, HG)], xsem.at[n + 4])
        pick(rim_a, rim_b, pl.ds(hn + HX, HG), oge.at[pl.ds(s * EXG + HG + BLK, HG)], xsem.at[n + 5])

    wcopies = []

    def row_of(z, x, c):
        return pl.multiple_of((z * 8 + x * 2 + c) * SHARD, SHARD)

    go(near, w.at[pl.ds(pl.multiple_of(zh * HALF, HALF), HALF)], wsem.at[32], wcopies)
    k = 0
    for d, (ra, rb) in enumerate(((ya0, yb0), (ya1, yb1), (ya2, yb2), (ya3, yb3))):
        col = pl.multiple_of(lax.rem(turn + 4 - d, 4) * QUART, QUART)
        for r in range(4):
            go(ra.at[pl.ds(r * SHARD, SHARD)], w.at[pl.ds(row_of(1 - zh, r, ci), SHARD), pl.ds(col, QUART)], wsem.at[k], wcopies)
            go(rb.at[pl.ds(r * SHARD, SHARD)], w.at[pl.ds(row_of(1 - zh, r, 1 - ci), SHARD), pl.ds(col, QUART)], wsem.at[k + 1], wcopies)
            k += 2

    red_ref[...] = jnp.zeros((PACK, 128), F32)
    for c in xcopies:
        c.wait()

    gain_row = dw[TAPS:TAPS + 1, :]
    bias_row = dw[TAPS + 1:TAPS + 2, :]

    def norm_step(i, carry):
        rows = pl.ds(pl.multiple_of(i * 128, 128), 128)
        v = xe[rows, :].astype(F32)
        mean = jnp.sum(v, axis=1, keepdims=True) * (1.0 / D)
        c = v - mean
        var = jnp.sum(c * c, axis=1, keepdims=True) * (1.0 / D)
        iv = lax.rsqrt(var + EPS)
        st = c * iv
        std[rows, :] = st
        inv[rows, :] = jnp.broadcast_to(iv, (128, 128))
        nrm[rows, :] = (st * gain_row + bias_row).astype(BF16)
        return carry

    lax.fori_loop(0, 2 * EXT // 128, norm_step, 0)

    for c in wcopies:
        c.wait()

    row384 = lax.broadcasted_iota(jnp.int32, (2 * EXT, 128), 0)
    second = row384 >= EXT
    t384 = pos * BLK + jnp.where(second, row384 - EXT + 32 * BLK, row384) - HX
    live384 = (t384 >= 0) & (t384 < length)
    iota16 = lax.broadcasted_iota(jnp.int32, (16, 128), 0)

    def chan_step(j, carry):
        col = pl.multiple_of(j * 256, 256)
        normed = nrm[...]
        a = jnp.dot(normed, w[:, pl.ds(col, 256)], preferred_element_type=F32)
        b = jnp.dot(normed, w[:, pl.ds(D + col, 256)], preferred_element_type=F32)
        sg = sigmoid(b)
        for h in range(2):
            ah = a[:, h * 128:(h + 1) * 128]
            sh = sg[:, h * 128:(h + 1) * 128]
            abuf[h] = ah
            sbuf[h] = sh
            gbuf[h] = jnp.where(live384, ah * sh, 0.0).astype(BF16).astype(F32)

        def tile_step(q, carry2):
            h = q // 2
            s = q % 2
            lane = pl.multiple_of((2 * j + h) * 128, 128)
            first = (pos + 32 * s) * BLK
            ext0 = s * EXT

            @pl.when(s == 0)
            def _():
                for k in range(TAPS):
                    kacc[k] = jnp.zeros((8, 128), F32)

            taps = [jnp.broadcast_to(dw[k:k + 1, pl.ds(lane, 128)], (8, 128)) for k in range(TAPS)]
            acc = {}
            done = {}
            for o in range(1, 8 * 19 + 32):
                v = gbuf[h, pl.ds(ext0 + o, 8), :]
                for i in range(20):
                    k = o - 1 - 8 * i
                    if 0 <= k < TAPS:
                        p = v * taps[k]
                        acc[i] = p if k == 0 else acc[i] + p
                        if k == TAPS - 1:
                            done[i] = acc.pop(i)
                            if i % 2 == 1:
                                m = i // 2
                                conv = jnp.concatenate([done.pop(i - 1), done.pop(i)], axis=0)
                                cs = sigmoid(conv)
                                t = iota16 + (first + 16 * m - HG)
                                live = (t >= 0) & (t < length)
                                og = oge[pl.ds(pl.multiple_of(s * EXG + 16 * m, 16), 16), pl.ds(lane, 128)].astype(F32)
                                av = conv * cs
                                sl = jnp.where(live, og * (cs + av * (1.0 - cs)), 0.0).astype(BF16).astype(F32)
                                slp[pl.ds(16 * m, 16), :] = sl
                                if 1 <= m <= 8:
                                    act_ref[pl.ds(pl.multiple_of(s * BLK + 16 * (m - 1), 16), 16), pl.ds(lane, 128)] = (
                                        jnp.where(live, av, 0.0).astype(BF16))

            ks = [kacc[k] for k in range(TAPS)]
            sv = {}
            for o in range(17, 17 + 8 * 15 + TAPS):
                v = gbuf[h, pl.ds(ext0 + o, 8), :]
                for i in range(16):
                    k = o - 17 - 8 * i
                    if 0 <= k < TAPS:
                        if k == 0:
                            sv[i] = slp[pl.ds(16 + 8 * i, 8), :]
                        ks[k] = ks[k] + v * sv[i]
            for k in range(TAPS):
                kacc[k] = ks[k]

            @pl.when(s == 1)
            def _():
                for k in range(TAPS):
                    red_ref[pl.ds((k // 8) * 8 * LT + k % 8 + (2 * j + h) * 8, 1), :] = jnp.sum(ks[k], axis=0, keepdims=True)

            acc = {}
            done = {}
            for o in range(1, 8 * 15 + 32):
                v = slp[pl.ds(o, 8), :]
                for i in range(16):
                    k = 31 + 8 * i - o
                    if 0 <= k < TAPS:
                        p = v * taps[k]
                        acc[i] = p if k == TAPS - 1 else acc[i] + p
                        if k == 0:
                            done[i] = acc.pop(i)
                            if i % 2 == 1:
                                m = i // 2
                                back = jnp.concatenate([done.pop(i - 1), done.pop(i)], axis=0)
                                t = iota16 + (first + 16 * m)
                                back = jnp.where(t < length, back, 0.0)
                                rows = pl.ds(pl.multiple_of(ext0 + HX + 16 * m, 16), 16)
                                av = abuf[h, rows, :]
                                sgv = sbuf[h, rows, :]
                                ga = back * sgv
                                out = pl.ds(pl.multiple_of(s * BLK + 16 * m, 16), 16)
                                gh[out, pl.ds(lane, 128)] = ga.astype(BF16)
                                gh[out, pl.ds(D + lane, 128)] = (ga * av * (1.0 - sgv)).astype(BF16)
            return carry2

        lax.fori_loop(0, 4, tile_step, 0)
        return carry

    lax.fori_loop(0, D // 256, chan_step, 0)

    act_copy = pltpu.make_async_copy(act_ref, act_hbm, xsem.at[12])
    act_copy.start()
    gn[...] = lax.dot_general(gh[...], w[...], (((1,), (1,)), ((), ())), preferred_element_type=F32)

    def grad_step(i, carry):
        gsum, bsum = carry
        src = pl.ds(pl.multiple_of(jnp.where(i >= 2, EXT - BLK, 0) + HX + i * 64, 32), 64)
        dst = pl.ds(pl.multiple_of(i * 64, 64), 64)
        g = gn[dst, :]
        st = std[src, :]
        gs = g * st
        for q in range(8):
            gsum = gsum + gs[q * 8:(q + 1) * 8]
            bsum = bsum + g[q * 8:(q + 1) * 8]
        sc_ = g * gain_row
        m1 = jnp.sum(sc_, axis=1, keepdims=True) * (1.0 / D)
        m2 = jnp.sum(sc_ * st, axis=1, keepdims=True) * (1.0 / D)
        iv = inv[src, 0:1]
        ig_ref[dst, :] = (iv * (sc_ - m1 - st * m2)).astype(BF16)
        return gsum, bsum

    zero = jnp.zeros((8, D), F32)
    gsum, bsum = lax.fori_loop(0, 4, grad_step, (zero, zero))
    grow = jnp.sum(gsum, axis=0, keepdims=True)
    brow = jnp.sum(bsum, axis=0, keepdims=True)
    for l in range(LT):
        red_ref[GAIN_ROW + l:GAIN_ROW + l + 1, :] = grow[:, l * 128:(l + 1) * 128]
        red_ref[BIAS_ROW + l:BIAS_ROW + l + 1, :] = brow[:, l * 128:(l + 1) * 128]
    act_copy.wait()


def run_fused(scalars, frames, out_grad, rim_a, rim_b, params, pieces):
    any_spec = pl.BlockSpec(memory_space=pltpu.HBM)
    vm = pl.BlockSpec(memory_space=pltpu.VMEM)
    return pl.pallas_call(
        fused,
        out_shape=(
            jax.ShapeDtypeStruct((2 * BLK, D), BF16),
            jax.ShapeDtypeStruct((2 * BLK, D), BF16),
            jax.ShapeDtypeStruct((PACK, 128), F32),
        ),
        in_specs=[pl.BlockSpec(memory_space=pltpu.SMEM)] + [any_spec] * 4 + [vm] + [any_spec] * len(pieces),
        out_specs=(any_spec, vm, vm),
        scratch_shapes=[
            pltpu.VMEM((2 * BLK, D), BF16),
            pltpu.VMEM((2 * EXT, D), BF16),
            pltpu.VMEM((2 * EXG, D), BF16),
            pltpu.VMEM((D, 2 * D), BF16),
            pltpu.VMEM((2 * EXT, D), BF16),
            pltpu.VMEM((2 * EXT, D), F32),
            pltpu.VMEM((2 * EXT, 128), F32),
            pltpu.VMEM((2, 2 * EXT, 128), F32),
            pltpu.VMEM((2, 2 * EXT, 128), F32),
            pltpu.VMEM((2, 2 * EXT, 128), F32),
            pltpu.VMEM((EXG, 128), F32),
            pltpu.VMEM((TAPS, 8, 128), F32),
            pltpu.VMEM((2 * BLK, 2 * D), BF16),
            pltpu.VMEM((2 * BLK, D), F32),
            pltpu.SemaphoreType.DMA((13,)),
            pltpu.SemaphoreType.DMA((40,)),
        ],
        compiler_params=pltpu.CompilerParams(vmem_limit_bytes=51 * 1024 * 1024),
        cost_estimate=pl.CostEstimate(flops=9_000_000_000, bytes_accessed=14_000_000, transcendentals=2_000_000),
    )(scalars, frames, out_grad, rim_a, rim_b, params, *pieces)


def take_rims(sc, x, g, near, far, sem):
    even = sc[5] == 0
    copies = []

    def go(src, dst):
        copies.append(pltpu.make_async_copy(src, dst, sem.at[len(copies)]))
        copies[-1].start()

    for s in range(2):
        last = s * BLK + BLK
        for dst, tail in ((near, even), (far, jnp.logical_not(even))):
            fx = pl.multiple_of(jnp.where(tail, last - HX, s * BLK), 16)
            fg = pl.multiple_of(jnp.where(tail, last - HG, s * BLK), 16)
            go(x.at[pl.ds(fx, HX)], dst.at[pl.ds(s * RIM, HX)])
            go(g.at[pl.ds(fg, HG)], dst.at[pl.ds(s * RIM + HX, HG)])
    for c in copies:
        c.wait()


def rims(scalars, x, g):
    any_spec = pl.BlockSpec(memory_space=pl.ANY)
    both = jax.ShapeDtypeStruct((2 * RIM, D), BF16)
    return pl.pallas_call(
        take_rims,
        out_shape=(both, both),
        in_specs=[pl.BlockSpec(memory_space=pltpu.SMEM), any_spec, any_spec],
        out_specs=(any_spec, any_spec),
        scratch_shapes=[pltpu.SemaphoreType.DMA((8,))],
        compiler_params=pltpu.CompilerParams(vmem_limit_bytes=1024 * 1024),
        cost_estimate=pl.CostEstimate(flops=0, bytes_accessed=1_200_000, transcendentals=0),
    )(scalars, x, g)


def write_copies(src, dst, sem):
    copies = [pltpu.make_async_copy(src, dst.at[i], sem.at[i]) for i in range(4)]
    for c in copies:
        c.start()
    for c in copies:
        c.wait()


def four_copies(part):
    any_spec = pl.BlockSpec(memory_space=pltpu.HBM)
    return pl.pallas_call(
        write_copies,
        out_shape=jax.ShapeDtypeStruct((4,) + part.shape, part.dtype),
        in_specs=[any_spec],
        out_specs=any_spec,
        scratch_shapes=[pltpu.SemaphoreType.DMA((4,))],
        compiler_params=pltpu.CompilerParams(vmem_limit_bytes=1024 * 1024),
        cost_estimate=pl.CostEstimate(flops=0, bytes_accessed=1_200_000, transcendentals=0),
    )(part)


def meet_next():
    pairs = []
    for i in range(1, 32, 2):
        pairs += [(i, (i + 1) % 32), ((i + 1) % 32, i)]
    return pairs


def gather_weight(own, turn, rim_a, rim_b, params):
    theirs = lax.rem(turn + 2, 4)
    quarter = lax.dynamic_slice_in_dim(own, theirs * QUART, QUART, axis=1)
    near = lax.all_gather(own, ("x", "core"), axis=0, tiled=True)
    far = lax.ppermute(quarter, ("zh", "zl"), [(i, 15 - i) for i in range(16)])
    far = four_copies(far)
    far, rim_a, rim_b, params = lax.optimization_barrier((far, rim_a, rim_b, params))
    a = lax.ppermute(rim_a, ("y", "zl"), [(i, i ^ 1) for i in range(32)])
    b = lax.ppermute(rim_b, ("y", "zl"), meet_next())
    far = lax.all_to_all(far, "x", 0, 0)
    far, a, b = lax.optimization_barrier((far, a, b))
    far = far.reshape(4 * SHARD, QUART)
    ya = [
        far,
        lax.ppermute(far, "y", shift(4, 1)),
        lax.ppermute(far, "zl", [(i, i ^ 1) for i in range(8)]),
        lax.ppermute(far, "y", shift(4, -1)),
    ]
    yb = [lax.ppermute(part, "core", shift(2, 1)) for part in ya]
    return a, b, params, [near] + ya + yb


def reduce_all(packed):
    plane = ("x", "core", "y")
    parts = lax.all_to_all(packed.reshape(32, PACK // 32, 128), plane, 0, 0)
    mine = jnp.sum(parts, axis=0)
    line = lax.all_to_all(jnp.broadcast_to(mine[None], (16,) + mine.shape), ("zh", "zl"), 0, 0)
    mine = jnp.sum(line, axis=0)
    whole = lax.all_to_all(jnp.broadcast_to(mine[None], (32,) + mine.shape), plane, 0, 0)
    whole = whole.reshape(PACK, 128)
    taps = whole[:GAIN_ROW].reshape(4, LT, 8, 128).transpose(0, 2, 1, 3).reshape(32, D)[:TAPS]
    return taps, whole[GAIN_ROW:GAIN_ROW + LT].reshape(D), whole[BIAS_ROW:BIAS_ROW + LT].reshape(D)


def on_device(frames, lengths, owner_map, norm_gain, norm_bias, proj_weight, dw_kernel, out_grad):
    idx = lax.axis_index
    x = frames.reshape(2 * BLK, D)
    dy = out_grad.reshape(2 * BLK, D)
    seq = idx("y") * 8 + idx("zl")
    position = jnp.mod(seq - owner_map[0, 0], 32)
    turn = lax.rem(idx("y") + 2 * lax.rem(idx("zl"), 2), 4)
    scalars = jnp.stack([position, lengths[0], idx("zh"), idx("core"), turn, lax.rem(idx("zl"), 2), position, position]).astype(jnp.int32)

    rim_a, rim_b = rims(scalars, x, dy)
    params = jnp.concatenate([dw_kernel, norm_gain[None], norm_bias[None]], axis=0)
    rim_a, rim_b, params, pieces = gather_weight(proj_weight, turn, rim_a, rim_b, params)
    act, ig, packed = run_fused(
        scalars, x, dy, rim_a, rim_b, params, pieces)
    kernel_grad, gain_grad, bias_grad = reduce_all(packed)
    return act.reshape(1, 2 * BLK, D), ig.reshape(1, 2 * BLK, D), kernel_grad, gain_grad, bias_grad


def solution(mesh):
    fine = Mesh(mesh.devices.reshape(2, 4, 2, 4, 8), ("zh", "x", "core", "y", "zl"))
    dp, seq = ("zh", "x", "core"), ("y", "zl")
    return jax.shard_map(
        on_device,
        mesh=fine,
        in_specs=(P(dp, seq, None), P(dp), P(dp, None), P(), P(), P(dp, None), P(), P(dp, seq, None)),
        out_specs=(P(dp, seq, None), P(dp, seq, None), P(), P(), P()),
        check_vma=False,
    )
```
